32 devices in a mesh: cohort: 2 (over y), people: 4 (over z), markers: 4 (over x, core).
Axes of the slice: x: 2, y: 2, z: 4, core: 2. Of those that a mesh axis runs over, the one named last changes fastest.
Arguments:
- genotype: int32 [12288, 2048], P(('cohort', 'people'), 'markers'), parts along dimension 0, may hold values from 0 to 170, as said below
- allele_freq: float32 [16384], P(('cohort', 'markers')), parts along dimension 0, may hold values from 0.05 to 0.5
- person_weight: float32 [12288], P(('cohort', 'people')), parts along dimension 0, may hold values from 0.5 to 18, as said below
- basis: bfloat16 [64, 8192], P('cohort', 'markers'), parts along dimension 0, may hold values from -0.0625 to 0.0625
- residuals: bfloat16 [128, 6144], P('cohort', 'people'), parts along dimension 0, may hold values from -6 to 6
- block_markers: int32 [2048], P('markers'), may hold values from 0 to 8191, as said below
Outputs:
- components: float32 [64, 6144], P('cohort', 'people'), parts along dimension 0
- coefficients: float32 [64, 64], P('cohort'), parts along dimension 0
- basis_next: float32 [4, 64, 2048], P('markers', 'cohort', 'people'), parts along dimension 1
- scores: float32 [4, 128, 512], P('markers', 'cohort', 'people'), parts along dimension 1
The draws below stay inside these ranges and needn't reach their ends.
There are 2 independent parts, one for each index of `cohort`. The reference program is written for one: setup_inputs(seed, part) draws one part's arguments, and reference() takes and returns one part's arrays. A program takes and returns all parts, laid end to end along the dimension named above; an argument that names none is the same for every part. Nothing has to cross between parts.
Inputs may be any that keep to these rules, and one draw needn't show every extreme that they name: `genotype`: each word packs the dosages (0, 1 or 2) of four consecutive markers of one person, marker 4 w + j in bits 2 j and 2 j + 1. `block_markers`: the j-th run of 512 entries holds distinct increasing markers among j * 2048 to (j + 1) * 2048 - 1, always including both of these ends. `person_weight`: positive weights.
All inputs are finite; a program needn't handle non-finite values.
Results may differ from the reference program's by a relative error of at most 0.0054.
Values sent between devices are 32-bit elements; how exact they have to be, the bound alone decides.
A program may use at most 128 MiB of HBM per device.

```python
import math
import jax
import jax.numpy as jnp
from jax import lax

K = 32
R = 64
P_DEV = 1536
M_DEV = 2048
MB_DEV = 512
PEOPLE = 6144
MARKERS = 8192
BLOCK = 2048
N_PEOPLE = 4
N_MARKERS = 4


def draw_genotype(key, part):
    number = jax.random.randint(key, (PEOPLE, MARKERS // 4), 0, 81)
    first = number % 3
    second = number // 3 % 3
    third = number // 9 % 3
    fourth = number // 27
    return (first + 4 * second + 16 * third + 64 * fourth).astype(jnp.int32)


def draw_person_weight(key, part):
    ramp = jnp.arange(PEOPLE, dtype=jnp.float32) / float(PEOPLE - 1)
    rough = jnp.exp(jax.random.uniform(key, (PEOPLE,), jnp.float32, -0.69, 0.69))
    values = jnp.exp(ramp * jnp.log(3.0)) * rough
    return values.astype(jnp.float32)


def draw_block_markers(key, part):
    shard_count = MARKERS // M_DEV
    keys = jax.random.split(key, shard_count)

    def one_shard(shard_key):
        inner = jax.random.permutation(shard_key, M_DEV - 2) + 1
        picked = jnp.sort(inner[:MB_DEV - 2])
        ends_low = jnp.zeros((1,), jnp.int32)
        ends_high = jnp.full((1,), M_DEV - 1, jnp.int32)
        return jnp.concatenate([ends_low, picked.astype(jnp.int32), ends_high])
    local = jax.vmap(one_shard)(keys)
    offsets = (jnp.arange(shard_count, dtype=jnp.int32) * M_DEV)[:, None]
    return (local + offsets).reshape(shard_count * MB_DEV).astype(jnp.int32)


def levels(rng, shape, cuts, smallest, largest):
    def one(axis_at, parts):
        draws = jax.random.uniform(jax.random.fold_in(jax.random.fold_in(rng, 6), axis_at), (parts,), jnp.float32, smallest / len(cuts), largest / len(cuts))
        return jnp.repeat(jnp.exp(draws), shape[axis_at] // parts).reshape((-1,) + (1,) * (len(shape) - axis_at - 1))

    gain = one(*cuts[0])
    for cut in cuts[1:]:
        gain = gain * one(*cut)
    return gain


def noise(key, dims, deviation, most, pieces=(), kind=jnp.bfloat16):
    drawn = deviation * jax.random.normal(key, dims, jnp.float32)
    if pieces:
        drawn = drawn * levels(key, dims, pieces, -0.22, 0.18)
    return jnp.clip(drawn, -most, most).astype(kind)


def setup_inputs(seed: int = 0, part: int = 0) -> dict:
    streams_of = jax.random.split(jax.random.key(seed), 7)
    part_keys = jax.random.split(jax.random.fold_in(streams_of[6], part), 7)
    genotype = draw_genotype(jax.random.fold_in(jax.random.fold_in(streams_of[6], part), 71), part)
    allele_freq = jnp.clip(0.05 + 0.45 * jax.random.uniform(part_keys[1], (MARKERS,), jnp.float32) ** levels(part_keys[1], (MARKERS,), ((0, 4),), -0.2, 0.2), 0.05, 0.5)
    person_weight = draw_person_weight(jax.random.fold_in(jax.random.fold_in(streams_of[6], part), 71), part)
    basis = noise(part_keys[3], (K, MARKERS), MARKERS ** -0.5, 0.0625, ((1, 4),))
    residuals = noise(part_keys[4], (R, PEOPLE), 1.0, 6.0, ((1, 4),))
    block_markers = draw_block_markers(jax.random.fold_in(streams_of[6], 71), part)
    return {"genotype": genotype, "allele_freq": allele_freq, "person_weight": person_weight, "basis": basis, "residuals": residuals, "block_markers": block_markers}


def decode(packed, freq, weight):
    shifts = 2 * jnp.arange(4, dtype=jnp.int32)
    dosage = jnp.bitwise_and(jnp.right_shift(packed[:, :, None], shifts[None, None, :]), 3)
    dosage = dosage.reshape(packed.shape[0], packed.shape[1] * 4).astype(jnp.float32)
    standard = (dosage - 2.0 * freq[None, :]) / jnp.sqrt(2.0 * freq * (1.0 - freq))[None, :]
    return (weight[:, None] * standard).astype(jnp.bfloat16)

def reference(genotype, allele_freq, person_weight, basis, residuals, block_markers):
    packed_blocks = genotype.reshape(N_PEOPLE, P_DEV, MARKERS // 4)
    weight_blocks = person_weight.reshape(N_PEOPLE, P_DEV)

    def sketch_block(inputs):
        weighted = decode(inputs[0], allele_freq, inputs[1])
        return jnp.dot(basis.astype(jnp.float32), weighted.T.astype(jnp.float32), preferred_element_type=jnp.float32)
    sketch_parts = lax.map(sketch_block, (packed_blocks, weight_blocks))
    sketch = jnp.transpose(sketch_parts, (1, 0, 2)).reshape(K, PEOPLE)
    gram_matrix = jnp.dot(sketch, sketch.T, precision=lax.Precision.HIGHEST)
    factor_low = jnp.linalg.cholesky(gram_matrix)
    ortho = jax.scipy.linalg.solve_triangular(factor_low, sketch, lower=True)
    resid_float = residuals.astype(jnp.float32)
    coefficients = jnp.dot(ortho, resid_float.T, precision=lax.Precision.HIGHEST)
    projected = (resid_float - jnp.dot(coefficients.T, ortho, precision=lax.Precision.HIGHEST)).astype(jnp.bfloat16)
    ortho_half = ortho.astype(jnp.bfloat16)
    ortho_blocks = jnp.transpose(ortho_half.reshape(K, N_PEOPLE, P_DEV), (1, 0, 2))
    proj_blocks = jnp.transpose(projected.reshape(R, N_PEOPLE, P_DEV), (1, 0, 2))

    def accumulate(carry, inputs):
        basis_acc, score_acc = carry
        weighted = decode(inputs[0], allele_freq, inputs[1])
        basis_acc = basis_acc + jnp.dot(inputs[2].astype(jnp.float32), weighted.astype(jnp.float32), preferred_element_type=jnp.float32)
        chosen = jnp.take(weighted, block_markers, axis=1)
        score_acc = score_acc + jnp.dot(inputs[3].astype(jnp.float32), chosen.astype(jnp.float32), preferred_element_type=jnp.float32)
        return ((basis_acc, score_acc), 0)
    start = (jnp.zeros((K, MARKERS), jnp.float32), jnp.zeros((R, BLOCK), jnp.float32))
    (basis_acc, score_acc), unused = lax.scan(accumulate, start, (packed_blocks, weight_blocks, ortho_blocks, proj_blocks))
    basis_next = jnp.transpose(basis_acc.reshape(K, N_MARKERS, M_DEV), (1, 0, 2))
    scores = jnp.transpose((score_acc / math.sqrt(PEOPLE)).reshape(R, N_MARKERS, MB_DEV), (1, 0, 2))
    components = math.sqrt(PEOPLE) * ortho
    return (components, coefficients, basis_next, scores)
```

```python
import functools
import math

import jax
import jax.numpy as jnp
from jax import lax
from jax.experimental import pallas as pl
from jax.experimental.pallas import tpu as pltpu
from jax.sharding import PartitionSpec as P

MESH = pl.DeviceIdType.MESH


def from_partner(block, axis, apart):
    count = lax.axis_size(axis)
    route = []
    for low in range(count):
        high = low | 1 << apart
        if high != low and high < count:
            route += [(low, high), (high, low)]
    return lax.ppermute(block, axis, route)


def decode(packed, freq, weight):
    shifts = 2 * jnp.arange(4, dtype=jnp.int32)
    dosage = jnp.bitwise_and(jnp.right_shift(packed[:, :, None], shifts[None, None, :]), 3)
    dosage = dosage.reshape(packed.shape[0], packed.shape[1] * 4).astype(jnp.float32)
    standard = (dosage - 2.0 * freq[None, :]) / jnp.sqrt(2.0 * freq * (1.0 - freq))[None, :]
    return (weight[:, None] * standard).astype(jnp.bfloat16)


def shards(genotype, allele_freq, person_weight, basis, residuals, block_markers):
    weighted = decode(genotype, allele_freq, person_weight)
    rows_here = weighted.shape[0]
    marker_cols = weighted.shape[1]
    marker_count = lax.axis_size("markers")
    marker_index = lax.axis_index("markers")
    share_rows = rows_here // marker_count
    partial_value = lax.dot_general(
        basis, weighted, (((1,), (1,)), ((), ())), preferred_element_type=jnp.float32
    )
    full_sketch = lax.psum(partial_value, "markers")
    own_sketch = lax.dynamic_slice_in_dim(full_sketch, marker_index * share_rows, share_rows, 1)
    own_residual = lax.dynamic_slice_in_dim(
        residuals, marker_index * share_rows, share_rows, 1
    ).astype(jnp.float32)
    gram_local = jnp.dot(own_sketch, own_sketch.T, precision=lax.Precision.HIGHEST)
    factor_up = jnp.linalg.cholesky(gram_local).T
    levels = lax.axis_size(("people", "markers")).bit_length() - 1
    for level in range(levels):
        partner = from_partner(factor_up, ("people", "markers"), level)
        combined = jnp.dot(factor_up.T, factor_up, precision=lax.Precision.HIGHEST) + jnp.dot(
            partner.T, partner, precision=lax.Precision.HIGHEST
        )
        factor_up = jnp.linalg.cholesky(combined).T
    factor_low = factor_up.T
    ortho = jax.scipy.linalg.solve_triangular(factor_low, full_sketch, lower=True)
    ortho_share = lax.dynamic_slice_in_dim(ortho, marker_index * share_rows, share_rows, 1)
    coefficients = lax.psum(
        jnp.dot(ortho_share, own_residual.T, precision=lax.Precision.HIGHEST), ("people", "markers")
    )
    projected = (
        residuals.astype(jnp.float32)
        - jnp.dot(coefficients.T, ortho, precision=lax.Precision.HIGHEST)
    ).astype(jnp.bfloat16)
    ortho_half = ortho.astype(jnp.bfloat16)
    basis_partial = jnp.dot(ortho_half, weighted, preferred_element_type=jnp.float32)
    columns = block_markers - marker_index * marker_cols
    chosen = jnp.take(weighted, columns, axis=1)
    score_partial = jnp.dot(projected, chosen, preferred_element_type=jnp.float32)
    people_count = lax.axis_size("people")
    people_index = lax.axis_index("people")
    basis_total, score_total = lax.psum((basis_partial, score_partial), "people")
    basis_width = basis_total.shape[1] // people_count
    score_width = score_total.shape[1] // people_count
    basis_own = lax.dynamic_slice_in_dim(basis_total, people_index * basis_width, basis_width, 1)
    score_own = lax.dynamic_slice_in_dim(score_total, people_index * score_width, score_width, 1)
    total_people = rows_here * people_count
    root_people = math.sqrt(total_people)
    components = root_people * ortho
    scores = (score_own / root_people)[None]
    return (components, coefficients, basis_own[None], scores)


ROWS_STEP = 128
TILE = 128


def split3(value):
    first = value.astype(jnp.bfloat16)
    left = value - first.astype(jnp.float32)
    second = left.astype(jnp.bfloat16)
    third = (left - second.astype(jnp.float32)).astype(jnp.bfloat16)
    return jnp.concatenate([first, second, third], axis=0)


def sum3(value):
    third = value.shape[0] // 3
    return value[:third] + value[third : 2 * third] + value[2 * third :]


def mm(left, right):
    return jnp.dot(left, right, preferred_element_type=jnp.float32)


def mm_nt(left, right, precision=None):
    return lax.dot_general(
        left,
        right,
        (((1,), (1,)), ((), ())),
        preferred_element_type=jnp.float32,
        precision=precision,
    )


def eliminate(full, count):
    rows = lax.broadcasted_iota(jnp.int32, full.shape, 0)
    lanes = lax.broadcasted_iota(jnp.int32, full.shape, 1)
    for k in range(count):
        column = jnp.broadcast_to(full[:, k : k + 1], full.shape)
        row = full[k : k + 1, :] * (1.0 / column[k : k + 1, :])
        full = jnp.where(rows > k, full - column * row, full)
    pivots = jnp.sum(jnp.where(rows == lanes, full, 0.0), axis=1, keepdims=True)
    return full * (1.0 / jnp.sqrt(pivots))


def kernel(
    root_people,
    geno_hbm,
    freq_hbm,
    weight_hbm,
    basis_hbm,
    resid_hbm,
    block_hbm,
    comp_ref,
    coef_ref,
    next_ref,
    score_ref,
    geno,
    freq_ref,
    weight_ref,
    basis_ref,
    resid_ref,
    block_ref,
    wt,
    hot,
    perm,
    freq_rows,
    basis_rows,
    part,
    part_in,
    sketch_all,
    resid_score,
    resid_score_in,
    gram_all,
    next_part,
    next_in,
    chosen_part,
    chosen_in,
    geno_sem,
    load_sem,
    send_sem,
    recv_sem,
):
    people = lax.axis_index("people")
    markers = lax.axis_index("markers")
    n = 4
    k_count, share = part.shape[1], part.shape[2]
    block = wt.shape[2]
    words = block // 4
    marker_peer = [lax.rem(markers + d, n) for d in range(n)]
    people_peer = [lax.rem(people + d, n) for d in range(n)]
    order = [1, 2, 3, 0]

    small = []
    for i, (src, dst) in enumerate(
        (
            (freq_hbm, freq_ref),
            (basis_hbm, basis_ref),
            (weight_hbm, weight_ref),
            (block_hbm, block_ref),
            (resid_hbm, resid_ref),
        )
    ):
        small.append(pltpu.make_async_copy(src, dst, load_sem.at[i]))
        small[-1].start()
    for step, d in enumerate(order):
        at = pl.ds(pl.multiple_of(marker_peer[d] * share, share), share)
        pltpu.make_async_copy(geno_hbm.at[at], geno.at[at], geno_sem.at[step]).start()

    barrier = pltpu.get_barrier_semaphore()
    for d in range(1, n):
        pl.semaphore_signal(
            barrier, inc=1, device_id={"markers": marker_peer[d]}, device_id_type=MESH
        )
        pl.semaphore_signal(
            barrier, inc=1, device_id={"people": people_peer[d]}, device_id_type=MESH
        )

    sends = {}

    def send(group, d, src, dst, axis):
        peer = marker_peer[d] if axis == "markers" else people_peer[d]
        copy = pltpu.make_async_remote_copy(
            src_ref=src,
            dst_ref=dst,
            send_sem=send_sem.at[group, d - 1],
            recv_sem=recv_sem.at[group, d - 1],
            device_id={axis: peer},
            device_id_type=MESH,
        )
        copy.start()
        sends[group, d] = copy

    marker = lax.broadcasted_iota(jnp.int32, (block, block), 0)
    place = lax.broadcasted_iota(jnp.int32, (block, block), 1)
    perm[...] = jnp.where(
        marker == 4 * lax.rem(place, words) + lax.div(place, words), 1.0, 0.0
    ).astype(jnp.bfloat16)
    small[0].wait()
    small[1].wait()
    small[2].wait()
    freq = jnp.concatenate([freq_ref[:, c * block : (c + 1) * block] for c in range(n)], axis=0)
    freq = jnp.concatenate([freq, freq], axis=0)
    freq = sum3(mm(split3(freq), perm[...]))[:n]
    freq_rows[0:n, :] = 2.0 * freq
    freq_rows[n : 2 * n, :] = 1.0 / jnp.sqrt(2.0 * freq * (1.0 - freq))
    basis = jnp.concatenate([basis_ref[:, c * block : (c + 1) * block] for c in range(n)], axis=0)
    basis_rows[...] = mm(basis, perm[...]).astype(jnp.bfloat16)

    pl.semaphore_wait(barrier, 2 * (n - 1))

    def share_copy(slot, target):
        return pltpu.make_async_remote_copy(
            src_ref=part.at[target],
            dst_ref=part_in.at[slot],
            send_sem=send_sem.at[0, slot],
            recv_sem=recv_sem.at[0, slot],
            device_id={"markers": target},
            device_id_type=MESH,
        )

    def decode(step, carry):
        target = lax.rem(markers + step + 1, n)
        at = pl.ds(pl.multiple_of(target * share, share), share)
        pltpu.make_async_copy(geno_hbm.at[at], geno.at[at], geno_sem.at[step]).wait()
        weight = []
        for i in range(share // ROWS_STEP):
            line = weight_ref[pl.ds(target * (share // ROWS_STEP) + i, 1), :]
            weight.append(jnp.transpose(jnp.broadcast_to(line, (ROWS_STEP, TILE))))
        weight = jnp.concatenate(weight, axis=0)
        total = None
        for c in range(n):
            packed = geno[at, c * words : (c + 1) * words]
            tiles = []
            for j in range(4):
                cols = slice(j * words, (j + 1) * words)
                dosage = jnp.bitwise_and(jnp.right_shift(packed, 2 * j), 3).astype(jnp.float32)
                value = (dosage - freq_rows[c : c + 1, cols]) * freq_rows[n + c : n + c + 1, cols]
                tiles.append((weight * value).astype(jnp.bfloat16))
            tile = jnp.concatenate(tiles, axis=1)
            wt[c, at, :] = tile
            got = mm_nt(basis_rows[c * k_count : (c + 1) * k_count, :], tile)
            total = got if total is None else total + got
        part[target] = total

        @pl.when(step < n - 1)
        def _():
            share_copy(step, target).start()

        return carry

    lax.fori_loop(0, n, decode, 0)
    for d in range(1, n):
        sends[0, d] = share_copy(d - 1, marker_peer[d])

    small[3].wait()
    small[4].wait()
    local = block_ref[...] - markers * (n * block)
    inner = lax.rem(local, block)
    column = lax.div(local, block) * block + lax.rem(inner, 4) * words + lax.div(inner, 4)
    for c in range(n):
        row = lax.broadcasted_iota(jnp.int32, (block, hot.shape[2]), 0) + c * block
        hot[c] = jnp.where(row == column, 1.0, 0.0).astype(jnp.bfloat16)

    for d in range(1, n):
        sends[0, d].wait_recv()
    sketch_all[markers] = part[markers] + part_in[0] + part_in[1] + part_in[2]
    for d in range(1, n):
        send(1, d, sketch_all.at[markers], sketch_all.at[markers], "markers")

    resid = resid_ref[...]
    picked = None
    for c in range(n):
        got = mm(split3(mm(resid, wt[c])), hot[c])
        picked = got if picked is None else picked + got
    picked = sum3(picked)
    width = picked.shape[1] // n
    for c in range(n):
        resid_score[c] = picked[:, c * width : (c + 1) * width]
    for d in range(1, n):
        send(2, d, resid_score.at[people_peer[d]], resid_score_in.at[d - 1], "people")

    for d in range(1, n):
        sends[1, d].wait_recv()
    sketch = jnp.concatenate([sketch_all[c] for c in range(n)], axis=1)
    both = jnp.concatenate([sketch, resid.astype(jnp.float32)], axis=0)
    gram = mm_nt(sketch, both, lax.Precision.HIGHEST)
    pad = jnp.zeros((k_count, TILE - gram.shape[1]), jnp.float32)
    gram_all[people] = jnp.concatenate([gram, pad], axis=1)
    for d in range(1, n):
        send(3, d, gram_all.at[people], gram_all.at[people], "people")

    pieces = split3(sketch)
    picked = None
    for d in (2, 1, 3, 0):
        c = people_peer[d]
        total = sum3(mm(pieces, wt[c]))
        next_part[c] = total
        if d:
            send(4, d, next_part.at[c], next_in.at[d - 1], "people")
        got = mm(split3(total), hot[c])
        picked = got if picked is None else picked + got
    picked = sum3(picked)
    for c in range(n):
        chosen_part[c] = picked[:, c * width : (c + 1) * width]
    for d in range(1, n):
        send(5, d, chosen_part.at[people_peer[d]], chosen_in.at[d - 1], "people")

    for d in range(1, n):
        sends[3, d].wait_recv()
    full = gram_all[0] + gram_all[1] + gram_all[2] + gram_all[3]
    lane = lax.broadcasted_iota(jnp.int32, full.shape, 1)
    line = lax.broadcasted_iota(jnp.int32, full.shape, 0)
    full = jnp.where(lane == line + (TILE - k_count), 1.0, full)
    full = eliminate(full, k_count)
    coef = full[:, k_count : TILE - k_count]
    inverse = full[:, TILE - k_count :]
    coef_ref[...] = coef
    comp_ref[...] = root_people * jnp.dot(
        inverse, sketch, preferred_element_type=jnp.float32, precision=lax.Precision.HIGHEST
    )

    for d in range(1, n):
        sends[2, d].wait_recv()
        sends[4, d].wait_recv()
        sends[5, d].wait_recv()
    total = next_part[people] + next_in[0] + next_in[1] + next_in[2]
    chosen = chosen_part[people] + chosen_in[0] + chosen_in[1] + chosen_in[2]
    scored = resid_score[people] + resid_score_in[0] + resid_score_in[1] + resid_score_in[2]
    solved = jnp.dot(
        inverse,
        jnp.concatenate([total, chosen], axis=1),
        preferred_element_type=jnp.float32,
        precision=lax.Precision.HIGHEST,
    )
    next_ref[0] = sum3(mm_nt(split3(solved[:, :block]), perm[...]))
    removed = lax.dot_general(
        coef,
        solved[:, block:],
        (((0,), (0,)), ((), ())),
        preferred_element_type=jnp.float32,
        precision=lax.Precision.HIGHEST,
    )
    score_ref[0] = (scored - removed) * (1.0 / root_people)
    for copy in sends.values():
        copy.wait_send()


def write_results(*refs):
    sources, results, store_sem = refs[:4], refs[4:8], refs[8]
    stores = [pltpu.make_async_copy(sources[i], results[i], store_sem.at[i]) for i in range(4)]
    for store in stores:
        store.start()
    for store in stores:
        store.wait()


def fused(genotype, allele_freq, person_weight, basis, residuals, block_markers):
    n = 4
    rows, words = genotype.shape
    k_count = basis.shape[0]
    r_count = residuals.shape[0]
    share = rows // n
    block = 4 * words // n
    picks = block_markers.shape[0]
    width = picks // n
    f32, bf16 = jnp.float32, jnp.bfloat16
    hbm = pl.BlockSpec(memory_space=pltpu.HBM)
    vmem = pl.BlockSpec(memory_space=pltpu.VMEM)
    root_people = math.sqrt(rows * n)
    shapes = (
        jax.ShapeDtypeStruct((k_count, rows), f32),
        jax.ShapeDtypeStruct((k_count, r_count), f32),
        jax.ShapeDtypeStruct((1, k_count, block), f32),
        jax.ShapeDtypeStruct((1, r_count, width), f32),
    )
    results = pl.pallas_call(
        functools.partial(kernel, root_people),
        out_shape=tuple(pltpu.VMEM(shape.shape, shape.dtype) for shape in shapes),
        in_specs=[hbm] * 6,
        out_specs=(vmem,) * 4,
        scratch_shapes=[
            pltpu.VMEM((rows, words), jnp.int32),
            pltpu.VMEM((1, n * block), f32),
            pltpu.VMEM((rows // TILE, TILE), f32),
            pltpu.VMEM(basis.shape, bf16),
            pltpu.VMEM(residuals.shape, bf16),
            pltpu.VMEM((1, picks), jnp.int32),
            pltpu.VMEM((n, rows, block), bf16),
            pltpu.VMEM((n, block, picks), bf16),
            pltpu.VMEM((block, block), bf16),
            pltpu.VMEM((2 * n, block), f32),
            pltpu.VMEM((n * k_count, block), bf16),
            pltpu.VMEM((n, k_count, share), f32),
            pltpu.VMEM((n - 1, k_count, share), f32),
            pltpu.VMEM((n, k_count, share), f32),
            pltpu.VMEM((n, r_count, width), f32),
            pltpu.VMEM((n - 1, r_count, width), f32),
            pltpu.VMEM((n, k_count, TILE), f32),
            pltpu.VMEM((n, k_count, block), f32),
            pltpu.VMEM((n - 1, k_count, block), f32),
            pltpu.VMEM((n, k_count, width), f32),
            pltpu.VMEM((n - 1, k_count, width), f32),
            pltpu.SemaphoreType.DMA((n,)),
            pltpu.SemaphoreType.DMA((5,)),
            pltpu.SemaphoreType.DMA((6, n - 1)),
            pltpu.SemaphoreType.DMA((6, n - 1)),
        ],
        compiler_params=pltpu.CompilerParams(
            collective_id=0, has_side_effects=True, vmem_limit_bytes=62 * 2**20
        ),
    )(
        genotype,
        allele_freq.reshape(1, -1),
        person_weight.reshape(-1, TILE),
        basis,
        residuals,
        block_markers.reshape(1, -1),
    )
    return pl.pallas_call(
        write_results,
        out_shape=shapes,
        in_specs=[vmem] * 4,
        out_specs=(hbm,) * 4,
        scratch_shapes=[pltpu.SemaphoreType.DMA((4,))],
    )(*[pltpu.with_memory_space_constraint(r, pltpu.VMEM) for r in results])


def solution(mesh):
    small = mesh.shape["people"] == 4 and mesh.shape["markers"] == 4
    placed = (
        P(("cohort", "people"), "markers"),
        P(("cohort", "markers")),
        P(("cohort", "people")),
        P("cohort", "markers"),
        P("cohort", "people"),
        P("markers"),
    )
    return jax.shard_map(
        fused if small else shards,
        mesh=mesh,
        in_specs=placed,
        out_specs=(
            P("cohort", "people"),
            P("cohort", None),
            P("markers", "cohort", "people"),
            P("markers", "cohort", "people"),
        ),
        check_vma=False,
    )
```

```python
import functools
import math

import jax
import jax.numpy as jnp
from jax import lax
from jax.experimental import pallas as pl
from jax.experimental.pallas import tpu as pltpu
from jax.sharding import PartitionSpec as P

MESH = pl.DeviceIdType.MESH


def from_partner(block, axis, apart):
    count = lax.axis_size(axis)
    route = []
    for low in range(count):
        high = low | 1 << apart
        if high != low and high < count:
            route += [(low, high), (high, low)]
    return lax.ppermute(block, axis, route)


def decode(packed, freq, weight):
    shifts = 2 * jnp.arange(4, dtype=jnp.int32)
    dosage = jnp.bitwise_and(jnp.right_shift(packed[:, :, None], shifts[None, None, :]), 3)
    dosage = dosage.reshape(packed.shape[0], packed.shape[1] * 4).astype(jnp.float32)
    standard = (dosage - 2.0 * freq[None, :]) / jnp.sqrt(2.0 * freq * (1.0 - freq))[None, :]
    return (weight[:, None] * standard).astype(jnp.bfloat16)


def shards(genotype, allele_freq, person_weight, basis, residuals, block_markers):
    weighted = decode(genotype, allele_freq, person_weight)
    rows_here = weighted.shape[0]
    marker_cols = weighted.shape[1]
    marker_count = lax.axis_size("markers")
    marker_index = lax.axis_index("markers")
    share_rows = rows_here // marker_count
    partial_value = lax.dot_general(
        basis, weighted, (((1,), (1,)), ((), ())), preferred_element_type=jnp.float32
    )
    full_sketch = lax.psum(partial_value, "markers")
    own_sketch = lax.dynamic_slice_in_dim(full_sketch, marker_index * share_rows, share_rows, 1)
    own_residual = lax.dynamic_slice_in_dim(
        residuals, marker_index * share_rows, share_rows, 1
    ).astype(jnp.float32)
    gram_local = jnp.dot(own_sketch, own_sketch.T, precision=lax.Precision.HIGHEST)
    factor_up = jnp.linalg.cholesky(gram_local).T
    levels = lax.axis_size(("people", "markers")).bit_length() - 1
    for level in range(levels):
        partner = from_partner(factor_up, ("people", "markers"), level)
        combined = jnp.dot(factor_up.T, factor_up, precision=lax.Precision.HIGHEST) + jnp.dot(
            partner.T, partner, precision=lax.Precision.HIGHEST
        )
        factor_up = jnp.linalg.cholesky(combined).T
    factor_low = factor_up.T
    ortho = jax.scipy.linalg.solve_triangular(factor_low, full_sketch, lower=True)
    ortho_share = lax.dynamic_slice_in_dim(ortho, marker_index * share_rows, share_rows, 1)
    coefficients = lax.psum(
        jnp.dot(ortho_share, own_residual.T, precision=lax.Precision.HIGHEST), ("people", "markers")
    )
    projected = (
        residuals.astype(jnp.float32)
        - jnp.dot(coefficients.T, ortho, precision=lax.Precision.HIGHEST)
    ).astype(jnp.bfloat16)
    ortho_half = ortho.astype(jnp.bfloat16)
    basis_partial = jnp.dot(ortho_half, weighted, preferred_element_type=jnp.float32)
    columns = block_markers - marker_index * marker_cols
    chosen = jnp.take(weighted, columns, axis=1)
    score_partial = jnp.dot(projected, chosen, preferred_element_type=jnp.float32)
    people_count = lax.axis_size("people")
    people_index = lax.axis_index("people")
    basis_total, score_total = lax.psum((basis_partial, score_partial), "people")
    basis_width = basis_total.shape[1] // people_count
    score_width = score_total.shape[1] // people_count
    basis_own = lax.dynamic_slice_in_dim(basis_total, people_index * basis_width, basis_width, 1)
    score_own = lax.dynamic_slice_in_dim(score_total, people_index * score_width, score_width, 1)
    total_people = rows_here * people_count
    root_people = math.sqrt(total_people)
    components = root_people * ortho
    scores = (score_own / root_people)[None]
    return (components, coefficients, basis_own[None], scores)


TILE = 128
PIECES = (512, 512, 256, 256)


def split2(value):
    first = value.astype(jnp.bfloat16)
    second = (value - first.astype(jnp.float32)).astype(jnp.bfloat16)
    return jnp.concatenate([first, second], axis=0)


def split3(value):
    first = value.astype(jnp.bfloat16)
    left = value - first.astype(jnp.float32)
    second = left.astype(jnp.bfloat16)
    third = (left - second.astype(jnp.float32)).astype(jnp.bfloat16)
    return jnp.concatenate([first, second, third], axis=0)


def sum2(value):
    half = value.shape[0] // 2
    return value[:half] + value[half:]


def sum3(value):
    third = value.shape[0] // 3
    return value[:third] + value[third : 2 * third] + value[2 * third :]


def mm(left, right):
    return jnp.dot(left, right, preferred_element_type=jnp.float32)


def mm_nt(left, right):
    return lax.dot_general(
        left, right, (((1,), (1,)), ((), ())), preferred_element_type=jnp.float32
    )


def exact(left, right):
    return jnp.dot(
        left, right, preferred_element_type=jnp.float32, precision=lax.Precision.HIGHEST
    )


def eliminate(full, count):
    rows = lax.broadcasted_iota(jnp.int32, full.shape, 0)
    lanes = lax.broadcasted_iota(jnp.int32, full.shape, 1)
    for k in range(count):
        column = jnp.broadcast_to(full[:, k : k + 1], full.shape)
        row = full[k : k + 1, :] * (1.0 / column[k : k + 1, :])
        full = jnp.where(rows > k, full - column * row, full)
    pivots = jnp.sum(jnp.where(rows == lanes, full, 0.0), axis=1, keepdims=True)
    return full * (1.0 / jnp.sqrt(pivots))


def kernel(
    root_people,
    geno_hbm,
    freq_hbm,
    weight_hbm,
    basis_hbm,
    resid_hbm,
    block_hbm,
    comp_ref,
    coef_ref,
    next_ref,
    score_ref,
    geno,
    freq_ref,
    weight_ref,
    basis_ref,
    resid_ref,
    block_ref,
    dose,
    hot,
    perm,
    freq_rows,
    basis_rows,
    part,
    core_in,
    chip_part,
    chip_in,
    sketch_half,
    resid_score,
    resid_score_in,
    gram_all,
    next_part,
    next_in,
    chosen_part,
    chosen_in,
    geno_sem,
    load_sem,
    pair_send,
    pair_recv,
    send_sem,
    recv_sem,
):
    people = lax.axis_index("people")
    markers = lax.axis_index("markers")
    n = 4
    half = part.shape[1]
    k_count = 2 * half
    block = dose.shape[2]
    words = block // 4
    core = lax.rem(markers, 2)
    core_peer = markers + 1 - 2 * core
    chip_peer = lax.rem(markers + 2, n)
    people_peer = [people, people + 1 - 2 * lax.rem(people, 2), lax.rem(people + 2, n), 3 - people]
    starts = [sum(PIECES[:i]) for i in range(len(PIECES))]
    spans = [pl.ds(start, size) for start, size in zip(starts, PIECES)]

    loads = []
    for i, span in enumerate(spans):
        loads.append(pltpu.make_async_copy(geno_hbm.at[span], geno.at[span], geno_sem.at[i]))
    small = [
        pltpu.make_async_copy(src, dst, load_sem.at[i])
        for i, (src, dst) in enumerate(
            (
                (freq_hbm, freq_ref),
                (basis_hbm, basis_ref),
                (weight_hbm, weight_ref),
                (block_hbm, block_ref),
                (resid_hbm, resid_ref),
            )
        )
    ]
    for load in small[:3] + loads + small[3:]:
        load.start()

    barrier = pltpu.get_barrier_semaphore()
    for peer in (core_peer, chip_peer):
        pl.semaphore_signal(barrier, inc=1, device_id={"markers": peer}, device_id_type=MESH)
    for d in (1, 2, 3):
        pl.semaphore_signal(
            barrier, inc=1, device_id={"people": people_peer[d]}, device_id_type=MESH
        )

    sends = {}

    def send(group, d, src, dst):
        copy = pltpu.make_async_remote_copy(
            src_ref=src,
            dst_ref=dst,
            send_sem=send_sem.at[group, d - 1],
            recv_sem=recv_sem.at[group, d - 1],
            device_id={"people": people_peer[d]},
            device_id_type=MESH,
        )
        copy.start()
        sends[group, d] = copy

    pairs = {}

    def pair(level, i):
        src, dst, peer = (
            (part.at[1 - core], core_in, core_peer),
            (chip_part, chip_in, chip_peer),
            (sketch_half.at[core], sketch_half.at[core], core_peer),
        )[level]
        copy = pltpu.make_async_remote_copy(
            src_ref=src.at[:, spans[i]],
            dst_ref=dst.at[:, spans[i]],
            send_sem=pair_send.at[level, i],
            recv_sem=pair_recv.at[level, i],
            device_id={"markers": peer},
            device_id_type=MESH,
        )
        copy.start()
        pairs[level, i] = copy

    place = lax.broadcasted_iota(jnp.int32, (1, block), 1)
    source = 4 * lax.rem(place, words) + lax.div(place, words)
    marker = lax.broadcasted_iota(jnp.int32, (block, block), 0)
    perm[...] = jnp.where(marker == source, 1.0, 0.0).astype(jnp.bfloat16)
    small[0].wait()
    small[1].wait()
    small[2].wait()
    freq = jnp.concatenate([freq_ref[:, c * block : (c + 1) * block] for c in range(n)], axis=0)
    freq = jnp.concatenate([freq, freq], axis=0)
    freq = sum3(mm(split3(freq), perm[...]))[:n]
    twice = 2.0 * freq
    scale = 1.0 / jnp.sqrt(2.0 * freq * (1.0 - freq))
    freq_rows[0:n, :] = twice
    freq_rows[n : 2 * n, :] = scale
    basis = jnp.concatenate([basis_ref[:, c * block : (c + 1) * block] for c in range(n)], axis=0)
    basis = mm(basis, perm[...])
    offset = jnp.zeros((k_count, 1), jnp.float32)
    for c in range(n):
        scaled = split2(basis[c * k_count : (c + 1) * k_count] * scale[c : c + 1])
        basis_rows[c] = scaled
        offset += jnp.sum(
            sum2(scaled.astype(jnp.float32)) * twice[c : c + 1], axis=1, keepdims=True
        )
    weight = jnp.concatenate(
        [weight_ref[i : i + 1, :] for i in range(weight_ref.shape[0])], axis=1
    )

    pl.semaphore_wait(barrier, 5)

    def forward(i):
        pairs[0, i].wait_recv()
        chip_part[:, spans[i]] = part[core, :, spans[i]] + core_in[:, spans[i]]
        pair(1, i)

    def finish(i):
        pairs[1, i].wait_recv()
        sketch_half[core, :, spans[i]] = chip_part[:, spans[i]] + chip_in[:, spans[i]]
        pair(2, i)

    for i, span in enumerate(spans):
        loads[i].wait()
        total = None
        for c in range(n):
            packed = geno[span, c * words : (c + 1) * words]
            tile = jnp.concatenate(
                [
                    jnp.bitwise_and(jnp.right_shift(packed, 2 * j), 3)
                    .astype(jnp.float32)
                    .astype(jnp.bfloat16)
                    for j in range(4)
                ],
                axis=1,
            )
            dose[c, span, :] = tile
            got = mm_nt(basis_rows[c], tile)
            total = got if total is None else total + got
        value = (sum2(total) - offset) * weight[:, starts[i] : starts[i] + PIECES[i]]
        part[0, :, span] = value[:half]
        part[1, :, span] = value[half:]
        pair(0, i)
        if i:
            forward(i - 1)

    small[3].wait()
    small[4].wait()
    local = block_ref[...] - markers * (n * block)
    inner = lax.rem(local, block)
    column = lax.div(local, block) * block + lax.rem(inner, 4) * words + lax.div(inner, 4)
    for c in range(n):
        row = lax.broadcasted_iota(jnp.int32, (block, hot.shape[2]), 0) + c * block
        hot[c] = jnp.where(row == column, 1.0, 0.0).astype(jnp.bfloat16)
    forward(len(PIECES) - 1)

    def center(raw, sums, c):
        return (raw - sums * freq_rows[c : c + 1, :]) * freq_rows[n + c : n + c + 1, :]

    resid = resid_ref[...]
    heavy = split2(resid.astype(jnp.float32) * weight)
    sums = sum2(jnp.sum(heavy.astype(jnp.float32), axis=1, keepdims=True))
    picked = None
    for c in range(n):
        value = center(sum2(mm(heavy, dose[c])), sums, c)
        got = mm(split2(value), hot[c])
        picked = got if picked is None else picked + got
    picked = sum2(picked)
    width = picked.shape[1] // n
    for c in range(n):
        resid_score[c] = picked[:, c * width : (c + 1) * width]
    for d in (2, 3, 1):
        send(0, d, resid_score.at[people_peer[d]], resid_score_in.at[d - 1])

    for i in range(len(PIECES)):
        finish(i)
    for i in range(len(PIECES)):
        pairs[2, i].wait_recv()
    sketch = jnp.concatenate([sketch_half[0], sketch_half[1]], axis=0)
    pieces = split3(sketch)
    gram = sum3(mm_nt(pieces, jnp.concatenate([pieces, resid], axis=0)))
    square = (
        gram[:, :k_count] + gram[:, k_count : 2 * k_count] + gram[:, 2 * k_count : 3 * k_count]
    )
    pad = jnp.zeros((k_count, k_count), jnp.float32)
    gram_all[people] = jnp.concatenate([square, gram[:, 3 * k_count :], pad], axis=1)
    for d in (2, 3, 1):
        send(1, d, gram_all.at[people], gram_all.at[people])

    heavy = split2(sketch * weight)
    sums = sum2(jnp.sum(heavy.astype(jnp.float32), axis=1, keepdims=True))
    picked = None
    for d in (2, 3, 1, 0):
        c = people_peer[d]
        freq_row = freq_rows[pl.ds(c, 1), :]
        scale_row = freq_rows[pl.ds(c + n, 1), :]
        total = (sum2(mm(heavy, dose[c])) - sums * freq_row) * scale_row
        next_part[c] = total
        if d:
            send(2, d, next_part.at[c], next_in.at[d - 1])
        got = mm(split2(total), hot[c])
        picked = got if picked is None else picked + got
    picked = sum2(picked)
    for c in range(n):
        chosen_part[c] = picked[:, c * width : (c + 1) * width]
    for d in (2, 3, 1):
        send(3, d, chosen_part.at[people_peer[d]], chosen_in.at[d - 1])

    for d in (1, 2, 3):
        sends[1, d].wait_recv()
    full = gram_all[0] + gram_all[1] + gram_all[2] + gram_all[3]
    lane = lax.broadcasted_iota(jnp.int32, full.shape, 1)
    line = lax.broadcasted_iota(jnp.int32, full.shape, 0)
    full = jnp.where(lane == line + (TILE - k_count), 1.0, full)
    full = eliminate(full, k_count)
    coef = full[:, k_count : TILE - k_count]
    inverse = full[:, TILE - k_count :]
    coef_ref[...] = coef
    comp_ref[...] = root_people * exact(inverse, sketch)
    remover = lax.dot_general(
        coef,
        inverse,
        (((0,), (0,)), ((), ())),
        preferred_element_type=jnp.float32,
        precision=lax.Precision.HIGHEST,
    )

    for group in (0, 2, 3):
        for d in (1, 2, 3):
            sends[group, d].wait_recv()
    total = next_part[people] + next_in[0] + next_in[1] + next_in[2]
    chosen = chosen_part[people] + chosen_in[0] + chosen_in[1] + chosen_in[2]
    scored = resid_score[people] + resid_score_in[0] + resid_score_in[1] + resid_score_in[2]
    solved = exact(inverse, total)
    next_ref[0] = sum3(mm_nt(split3(solved), perm[...]))
    score_ref[0] = (scored - exact(remover, chosen)) * (1.0 / root_people)
    for copy in list(pairs.values()) + list(sends.values()):
        copy.wait_send()


def write_results(*refs):
    sources, results, store_sem = refs[:4], refs[4:8], refs[8]
    stores = [pltpu.make_async_copy(sources[i], results[i], store_sem.at[i]) for i in range(4)]
    for store in stores:
        store.start()
    for store in stores:
        store.wait()


def fused(genotype, allele_freq, person_weight, basis, residuals, block_markers):
    n = 4
    rows, words = genotype.shape
    k_count = basis.shape[0]
    r_count = residuals.shape[0]
    block = 4 * words // n
    picks = block_markers.shape[0]
    width = picks // n
    f32, bf16 = jnp.float32, jnp.bfloat16
    hbm = pl.BlockSpec(memory_space=pltpu.HBM)
    vmem = pl.BlockSpec(memory_space=pltpu.VMEM)
    root_people = math.sqrt(rows * n)
    shapes = (
        jax.ShapeDtypeStruct((k_count, rows), f32),
        jax.ShapeDtypeStruct((k_count, r_count), f32),
        jax.ShapeDtypeStruct((1, k_count, block), f32),
        jax.ShapeDtypeStruct((1, r_count, width), f32),
    )
    results = pl.pallas_call(
        functools.partial(kernel, root_people),
        out_shape=tuple(pltpu.VMEM(shape.shape, shape.dtype) for shape in shapes),
        in_specs=[hbm] * 6,
        out_specs=(vmem,) * 4,
        scratch_shapes=[
            pltpu.VMEM((rows, words), jnp.int32),
            pltpu.VMEM((1, n * block), f32),
            pltpu.VMEM((rows // TILE, TILE), f32),
            pltpu.VMEM(basis.shape, bf16),
            pltpu.VMEM(residuals.shape, bf16),
            pltpu.VMEM((1, picks), jnp.int32),
            pltpu.VMEM((n, rows, block), bf16),
            pltpu.VMEM((n, block, picks), bf16),
            pltpu.VMEM((block, block), bf16),
            pltpu.VMEM((2 * n, block), f32),
            pltpu.VMEM((n, 2 * k_count, block), bf16),
            pltpu.VMEM((2, k_count // 2, rows), f32),
            pltpu.VMEM((k_count // 2, rows), f32),
            pltpu.VMEM((k_count // 2, rows), f32),
            pltpu.VMEM((k_count // 2, rows), f32),
            pltpu.VMEM((2, k_count // 2, rows), f32),
            pltpu.VMEM((n, r_count, width), f32),
            pltpu.VMEM((n - 1, r_count, width), f32),
            pltpu.VMEM((n, k_count, TILE), f32),
            pltpu.VMEM((n, k_count, block), f32),
            pltpu.VMEM((n - 1, k_count, block), f32),
            pltpu.VMEM((n, k_count, width), f32),
            pltpu.VMEM((n - 1, k_count, width), f32),
            pltpu.SemaphoreType.DMA((len(PIECES),)),
            pltpu.SemaphoreType.DMA((5,)),
            pltpu.SemaphoreType.DMA((3, len(PIECES))),
            pltpu.SemaphoreType.DMA((3, len(PIECES))),
            pltpu.SemaphoreType.DMA((4, n - 1)),
            pltpu.SemaphoreType.DMA((4, n - 1)),
        ],
        compiler_params=pltpu.CompilerParams(
            collective_id=0, has_side_effects=True, vmem_limit_bytes=62 * 2**20
        ),
    )(
        genotype,
        allele_freq.reshape(1, -1),
        person_weight.reshape(-1, TILE),
        basis,
        residuals,
        block_markers.reshape(1, -1),
    )
    return pl.pallas_call(
        write_results,
        out_shape=shapes,
        in_specs=[vmem] * 4,
        out_specs=(hbm,) * 4,
        scratch_shapes=[pltpu.SemaphoreType.DMA((4,))],
    )(*[pltpu.with_memory_space_constraint(r, pltpu.VMEM) for r in results])


def solution(mesh):
    small = mesh.shape["people"] == 4 and mesh.shape["markers"] == 4
    placed = (
        P(("cohort", "people"), "markers"),
        P(("cohort", "markers")),
        P(("cohort", "people")),
        P("cohort", "markers"),
        P("cohort", "people"),
        P("markers"),
    )
    return jax.shard_map(
        fused if small else shards,
        mesh=mesh,
        in_specs=placed,
        out_specs=(
            P("cohort", "people"),
            P("cohort", None),
            P("markers", "cohort", "people"),
            P("markers", "cohort", "people"),
        ),
        check_vma=False,
    )
```

```python
import functools
import math

import jax
import jax.numpy as jnp
from jax import lax
from jax.experimental import pallas as pl
from jax.experimental.pallas import tpu as pltpu
from jax.sharding import PartitionSpec as P

MESH = pl.DeviceIdType.MESH


def from_partner(block, axis, apart):
    count = lax.axis_size(axis)
    route = []
    for low in range(count):
        high = low | 1 << apart
        if high != low and high < count:
            route += [(low, high), (high, low)]
    return lax.ppermute(block, axis, route)


def decode(packed, freq, weight):
    shifts = 2 * jnp.arange(4, dtype=jnp.int32)
    dosage = jnp.bitwise_and(jnp.right_shift(packed[:, :, None], shifts[None, None, :]), 3)
    dosage = dosage.reshape(packed.shape[0], packed.shape[1] * 4).astype(jnp.float32)
    standard = (dosage - 2.0 * freq[None, :]) / jnp.sqrt(2.0 * freq * (1.0 - freq))[None, :]
    return (weight[:, None] * standard).astype(jnp.bfloat16)


def shards(genotype, allele_freq, person_weight, basis, residuals, block_markers):
    weighted = decode(genotype, allele_freq, person_weight)
    rows_here = weighted.shape[0]
    marker_cols = weighted.shape[1]
    marker_count = lax.axis_size("markers")
    marker_index = lax.axis_index("markers")
    share_rows = rows_here // marker_count
    partial_value = lax.dot_general(
        basis, weighted, (((1,), (1,)), ((), ())), preferred_element_type=jnp.float32
    )
    full_sketch = lax.psum(partial_value, "markers")
    own_sketch = lax.dynamic_slice_in_dim(full_sketch, marker_index * share_rows, share_rows, 1)
    own_residual = lax.dynamic_slice_in_dim(
        residuals, marker_index * share_rows, share_rows, 1
    ).astype(jnp.float32)
    gram_local = jnp.dot(own_sketch, own_sketch.T, precision=lax.Precision.HIGHEST)
    factor_up = jnp.linalg.cholesky(gram_local).T
    levels = lax.axis_size(("people", "markers")).bit_length() - 1
    for level in range(levels):
        partner = from_partner(factor_up, ("people", "markers"), level)
        combined = jnp.dot(factor_up.T, factor_up, precision=lax.Precision.HIGHEST) + jnp.dot(
            partner.T, partner, precision=lax.Precision.HIGHEST
        )
        factor_up = jnp.linalg.cholesky(combined).T
    factor_low = factor_up.T
    ortho = jax.scipy.linalg.solve_triangular(factor_low, full_sketch, lower=True)
    ortho_share = lax.dynamic_slice_in_dim(ortho, marker_index * share_rows, share_rows, 1)
    coefficients = lax.psum(
        jnp.dot(ortho_share, own_residual.T, precision=lax.Precision.HIGHEST), ("people", "markers")
    )
    projected = (
        residuals.astype(jnp.float32)
        - jnp.dot(coefficients.T, ortho, precision=lax.Precision.HIGHEST)
    ).astype(jnp.bfloat16)
    ortho_half = ortho.astype(jnp.bfloat16)
    basis_partial = jnp.dot(ortho_half, weighted, preferred_element_type=jnp.float32)
    columns = block_markers - marker_index * marker_cols
    chosen = jnp.take(weighted, columns, axis=1)
    score_partial = jnp.dot(projected, chosen, preferred_element_type=jnp.float32)
    people_count = lax.axis_size("people")
    people_index = lax.axis_index("people")
    basis_total, score_total = lax.psum((basis_partial, score_partial), "people")
    basis_width = basis_total.shape[1] // people_count
    score_width = score_total.shape[1] // people_count
    basis_own = lax.dynamic_slice_in_dim(basis_total, people_index * basis_width, basis_width, 1)
    score_own = lax.dynamic_slice_in_dim(score_total, people_index * score_width, score_width, 1)
    total_people = rows_here * people_count
    root_people = math.sqrt(total_people)
    components = root_people * ortho
    scores = (score_own / root_people)[None]
    return (components, coefficients, basis_own[None], scores)


TILE = 128
PIECES = (512, 512, 256, 256)


def split2(value):
    first = value.astype(jnp.bfloat16)
    second = (value - first.astype(jnp.float32)).astype(jnp.bfloat16)
    return jnp.concatenate([first, second], axis=0)


def split3(value):
    first = value.astype(jnp.bfloat16)
    left = value - first.astype(jnp.float32)
    second = left.astype(jnp.bfloat16)
    third = (left - second.astype(jnp.float32)).astype(jnp.bfloat16)
    return jnp.concatenate([first, second, third], axis=0)


def sum2(value):
    half = value.shape[0] // 2
    return value[:half] + value[half:]


def sum3(value):
    third = value.shape[0] // 3
    return value[:third] + value[third : 2 * third] + value[2 * third :]


def mm(left, right):
    return jnp.dot(left, right, preferred_element_type=jnp.float32)


def mm_nt(left, right):
    return lax.dot_general(
        left, right, (((1,), (1,)), ((), ())), preferred_element_type=jnp.float32
    )


def exact(left, right):
    return jnp.dot(
        left, right, preferred_element_type=jnp.float32, precision=lax.Precision.HIGHEST
    )


def eliminate(full, count):
    rows = lax.broadcasted_iota(jnp.int32, full.shape, 0)
    lanes = lax.broadcasted_iota(jnp.int32, full.shape, 1)
    for k in range(count):
        column = jnp.broadcast_to(full[:, k : k + 1], full.shape)
        row = full[k : k + 1, :] * (1.0 / column[k : k + 1, :])
        full = jnp.where(rows > k, full - column * row, full)
    pivots = jnp.sum(jnp.where(rows == lanes, full, 0.0), axis=1, keepdims=True)
    return full * (1.0 / jnp.sqrt(pivots))


def kernel(
    root_people,
    geno_hbm,
    freq_hbm,
    weight_hbm,
    basis_hbm,
    resid_hbm,
    block_hbm,
    comp_ref,
    coef_ref,
    next_ref,
    score_ref,
    geno,
    freq_ref,
    weight_ref,
    basis_ref,
    resid_ref,
    block_ref,
    dose,
    hot,
    perm,
    freq_rows,
    basis_rows,
    part,
    core_in,
    chip_part,
    chip_in,
    sketch_half,
    resid_score,
    resid_score_in,
    gram_part,
    gram_in,
    gram_sum,
    next_part,
    next_near,
    next_in,
    next_mine,
    next_pass,
    next_far,
    chosen_part,
    chosen_near,
    chosen_mine,
    chosen_pass,
    chosen_far,
    geno_sem,
    load_sem,
    pair_send,
    pair_recv,
    send_sem,
    recv_sem,
):
    people = lax.axis_index("people")
    markers = lax.axis_index("markers")
    n = 4
    half = part.shape[1]
    k_count = 2 * half
    block = dose.shape[2]
    words = block // 4
    core = lax.rem(markers, 2)
    core_peer = markers + 1 - 2 * core
    chip_peer = lax.rem(markers + 2, n)
    people_peer = [people, people + 1 - 2 * lax.rem(people, 2), lax.rem(people + 2, n), 3 - people]
    starts = [sum(PIECES[:i]) for i in range(len(PIECES))]
    spans = [pl.ds(start, size) for start, size in zip(starts, PIECES)]

    loads = []
    for i, span in enumerate(spans):
        loads.append(pltpu.make_async_copy(geno_hbm.at[span], geno.at[span], geno_sem.at[i]))
    small = [
        pltpu.make_async_copy(src, dst, load_sem.at[i])
        for i, (src, dst) in enumerate(
            (
                (freq_hbm, freq_ref),
                (basis_hbm, basis_ref),
                (weight_hbm, weight_ref),
                (block_hbm, block_ref),
                (resid_hbm, resid_ref),
            )
        )
    ]
    for load in small[:3] + loads + small[3:]:
        load.start()

    barrier = pltpu.get_barrier_semaphore()
    for peer in (core_peer, chip_peer):
        pl.semaphore_signal(barrier, inc=1, device_id={"markers": peer}, device_id_type=MESH)
    for d in (1, 2, 3):
        pl.semaphore_signal(
            barrier, inc=1, device_id={"people": people_peer[d]}, device_id_type=MESH
        )

    sends = {}

    def send(group, d, src, dst):
        copy = pltpu.make_async_remote_copy(
            src_ref=src,
            dst_ref=dst,
            send_sem=send_sem.at[group, d],
            recv_sem=recv_sem.at[group, d],
            device_id={"people": people_peer[d]} if d else {"markers": core_peer},
            device_id_type=MESH,
        )
        copy.start()
        sends[group, d] = copy

    pairs = {}

    def pair(level, i):
        src, dst, peer = (
            (part.at[1 - core], core_in, core_peer),
            (chip_part, chip_in, chip_peer),
            (sketch_half.at[core], sketch_half.at[core], core_peer),
        )[level]
        copy = pltpu.make_async_remote_copy(
            src_ref=src.at[:, spans[i]],
            dst_ref=dst.at[:, spans[i]],
            send_sem=pair_send.at[level, i],
            recv_sem=pair_recv.at[level, i],
            device_id={"markers": peer},
            device_id_type=MESH,
        )
        copy.start()
        pairs[level, i] = copy

    place = lax.broadcasted_iota(jnp.int32, (1, block), 1)
    source = 4 * lax.rem(place, words) + lax.div(place, words)
    marker = lax.broadcasted_iota(jnp.int32, (block, block), 0)
    perm[...] = jnp.where(marker == source, 1.0, 0.0).astype(jnp.bfloat16)
    small[0].wait()
    small[1].wait()
    small[2].wait()
    freq = jnp.concatenate([freq_ref[:, c * block : (c + 1) * block] for c in range(n)], axis=0)
    freq = jnp.concatenate([freq, freq], axis=0)
    freq = sum3(mm(split3(freq), perm[...]))[:n]
    twice = 2.0 * freq
    scale = 1.0 / jnp.sqrt(2.0 * freq * (1.0 - freq))
    freq_rows[0:n, :] = twice
    freq_rows[n : 2 * n, :] = scale
    basis = jnp.concatenate([basis_ref[:, c * block : (c + 1) * block] for c in range(n)], axis=0)
    basis = mm(basis, perm[...])
    offset = jnp.zeros((k_count, 1), jnp.float32)
    for c in range(n):
        scaled = (basis[c * k_count : (c + 1) * k_count] * scale[c : c + 1]).astype(jnp.bfloat16)
        basis_rows[c] = scaled
        offset += jnp.sum(
            scaled.astype(jnp.float32) * twice[c : c + 1], axis=1, keepdims=True
        )
    weight = jnp.concatenate(
        [weight_ref[i : i + 1, :] for i in range(weight_ref.shape[0])], axis=1
    )

    pl.semaphore_wait(barrier, 5)

    def forward(i):
        pairs[0, i].wait_recv()
        chip_part[:, spans[i]] = part[core, :, spans[i]] + core_in[:, spans[i]]
        pair(1, i)

    def finish(i):
        pairs[1, i].wait_recv()
        sketch_half[core, :, spans[i]] = chip_part[:, spans[i]] + chip_in[:, spans[i]]
        pair(2, i)

    for i, span in enumerate(spans):
        loads[i].wait()
        total = None
        for c in range(n):
            packed = geno[span, c * words : (c + 1) * words]
            tile = jnp.concatenate(
                [
                    jnp.bitwise_and(jnp.right_shift(packed, 2 * j), 3)
                    .astype(jnp.float32)
                    .astype(jnp.bfloat16)
                    for j in range(4)
                ],
                axis=1,
            )
            dose[c, span, :] = tile
            got = mm_nt(basis_rows[c], tile)
            total = got if total is None else total + got
        value = (total - offset) * weight[:, starts[i] : starts[i] + PIECES[i]]
        part[0, :, span] = value[:half]
        part[1, :, span] = value[half:]
        pair(0, i)
        if i:
            forward(i - 1)

    small[3].wait()
    small[4].wait()
    local = block_ref[...] - markers * (n * block)
    inner = lax.rem(local, block)
    column = lax.div(local, block) * block + lax.rem(inner, 4) * words + lax.div(inner, 4)
    for c in range(n):
        row = lax.broadcasted_iota(jnp.int32, (block, hot.shape[2]), 0) + c * block
        hot[c] = jnp.where(row == column, 1.0, 0.0).astype(jnp.bfloat16)
    forward(len(PIECES) - 1)

    def center(raw, sums, c):
        return (raw - sums * freq_rows[c : c + 1, :]) * freq_rows[n + c : n + c + 1, :]

    resid = resid_ref[...]
    heavy = split2(resid.astype(jnp.float32) * weight)
    sums = sum2(jnp.sum(heavy.astype(jnp.float32), axis=1, keepdims=True))
    picked = None
    for c in range(n):
        value = center(sum2(mm(heavy, dose[c])), sums, c)
        got = mm(split2(value), hot[c])
        picked = got if picked is None else picked + got
    picked = sum2(picked)
    width = picked.shape[1] // n
    for c in range(n):
        resid_score[c] = picked[:, c * width : (c + 1) * width]
    for d in (2, 3, 1):
        send(0, d, resid_score.at[people_peer[d]], resid_score_in.at[d - 1])

    for i in range(len(PIECES)):
        finish(i)
    for i in range(len(PIECES)):
        pairs[2, i].wait_recv()
    sketch = jnp.concatenate([sketch_half[0], sketch_half[1]], axis=0)
    heavy = split2(sketch * weight)
    sums = sum2(jnp.sum(heavy.astype(jnp.float32), axis=1, keepdims=True))
    cut = block // 2
    picked = None
    for d in (3, 2, 1, 0):
        c = people_peer[d]
        freq_row = freq_rows[pl.ds(c, 1), :]
        scale_row = freq_rows[pl.ds(c + n, 1), :]
        total = (sum2(mm(heavy, dose[c])) - sums * freq_row) * scale_row
        next_part[c, 0] = total[:, :cut]
        next_part[c, 1] = total[:, cut:]
        if d == 3:
            send(2, 1, next_part.at[c, 1], next_pass)
        if d > 1:
            send(2, d, next_part.at[c, 0], next_in.at[d - 2])
        got = mm(split2(total), hot[c])
        picked = got if picked is None else picked + got
        if d == 3:
            pieces = split3(sketch)
            gram = sum3(mm_nt(pieces, jnp.concatenate([pieces, resid], axis=0)))
            square = (
                gram[:, :k_count]
                + gram[:, k_count : 2 * k_count]
                + gram[:, 2 * k_count : 3 * k_count]
            )
            pad = jnp.zeros((k_count, k_count), jnp.float32)
            gram = jnp.concatenate([square, gram[:, 3 * k_count :], pad], axis=1)
            gram_part[0] = gram[:half]
            gram_part[1] = gram[half:]
            gram_in[people] = gram_part[core]
            for far in (3, 2, 1):
                send(1, far, gram_part.at[core], gram_in.at[people])
    picked = sum2(picked)
    for c in range(n):
        chosen_part[c] = picked[:, c * width : (c + 1) * width]
    send(4, 1, chosen_part.at[people_peer[3]], chosen_pass)
    send(5, 1, chosen_part.at[people_peer[1]], chosen_near)

    sends[2, 1].wait_recv()
    next_mine[...] = next_part[people_peer[2], 1] + next_pass[...]
    send(3, 2, next_mine, next_far)
    send(3, 1, next_part.at[people_peer[1]], next_near)
    for d in (1, 2, 3):
        sends[1, d].wait_recv()
    gram_sum[core] = gram_in[0] + gram_in[1] + gram_in[2] + gram_in[3]
    send(1, 0, gram_sum.at[core], gram_sum.at[core])
    sends[4, 1].wait_recv()
    chosen_mine[...] = chosen_part[people_peer[2]] + chosen_pass[...]
    send(4, 2, chosen_mine, chosen_far)
    sends[1, 0].wait_recv()
    full = jnp.concatenate([gram_sum[0], gram_sum[1]], axis=0)
    lane = lax.broadcasted_iota(jnp.int32, full.shape, 1)
    line = lax.broadcasted_iota(jnp.int32, full.shape, 0)
    full = jnp.where(lane == line + (TILE - k_count), 1.0, full)
    full = eliminate(full, k_count)
    coef = full[:, k_count : TILE - k_count]
    inverse = full[:, TILE - k_count :]
    coef_ref[...] = coef
    comp_ref[...] = root_people * exact(inverse, sketch)
    remover = lax.dot_general(
        coef,
        inverse,
        (((0,), (0,)), ((), ())),
        preferred_element_type=jnp.float32,
        precision=lax.Precision.HIGHEST,
    )

    for group, d in ((0, 1), (0, 2), (0, 3), (2, 2), (2, 3), (3, 1), (3, 2), (4, 2), (5, 1)):
        sends[group, d].wait_recv()
    total = next_part[people] + next_near[...]
    total = jnp.concatenate(
        [total[0] + next_in[0] + next_in[1], total[1] + next_far[...]], axis=1
    )
    chosen = chosen_part[people] + chosen_near[...] + chosen_far[...]
    scored = resid_score[people] + resid_score_in[0] + resid_score_in[1] + resid_score_in[2]
    solved = exact(inverse, total)
    next_ref[0] = sum3(mm_nt(split3(solved), perm[...]))
    score_ref[0] = (scored - exact(remover, chosen)) * (1.0 / root_people)
    for copy in list(pairs.values()) + list(sends.values()):
        copy.wait_send()


def write_results(*refs):
    sources, results, store_sem = refs[:4], refs[4:8], refs[8]
    stores = [pltpu.make_async_copy(sources[i], results[i], store_sem.at[i]) for i in range(4)]
    for store in stores:
        store.start()
    for store in stores:
        store.wait()


def fused(genotype, allele_freq, person_weight, basis, residuals, block_markers):
    n = 4
    rows, words = genotype.shape
    k_count = basis.shape[0]
    r_count = residuals.shape[0]
    block = 4 * words // n
    picks = block_markers.shape[0]
    width = picks // n
    f32, bf16 = jnp.float32, jnp.bfloat16
    hbm = pl.BlockSpec(memory_space=pltpu.HBM)
    vmem = pl.BlockSpec(memory_space=pltpu.VMEM)
    root_people = math.sqrt(rows * n)
    shapes = (
        jax.ShapeDtypeStruct((k_count, rows), f32),
        jax.ShapeDtypeStruct((k_count, r_count), f32),
        jax.ShapeDtypeStruct((1, k_count, block), f32),
        jax.ShapeDtypeStruct((1, r_count, width), f32),
    )
    results = pl.pallas_call(
        functools.partial(kernel, root_people),
        out_shape=tuple(pltpu.VMEM(shape.shape, shape.dtype) for shape in shapes),
        in_specs=[hbm] * 6,
        out_specs=(vmem,) * 4,
        scratch_shapes=[
            pltpu.VMEM((rows, words), jnp.int32),
            pltpu.VMEM((1, n * block), f32),
            pltpu.VMEM((rows // TILE, TILE), f32),
            pltpu.VMEM(basis.shape, bf16),
            pltpu.VMEM(residuals.shape, bf16),
            pltpu.VMEM((1, picks), jnp.int32),
            pltpu.VMEM((n, rows, block), bf16),
            pltpu.VMEM((n, block, picks), bf16),
            pltpu.VMEM((block, block), bf16),
            pltpu.VMEM((2 * n, block), f32),
            pltpu.VMEM((n, k_count, block), bf16),
            pltpu.VMEM((2, k_count // 2, rows), f32),
            pltpu.VMEM((k_count // 2, rows), f32),
            pltpu.VMEM((k_count // 2, rows), f32),
            pltpu.VMEM((k_count // 2, rows), f32),
            pltpu.VMEM((2, k_count // 2, rows), f32),
            pltpu.VMEM((n, r_count, width), f32),
            pltpu.VMEM((n - 1, r_count, width), f32),
            pltpu.VMEM((2, k_count // 2, TILE), f32),
            pltpu.VMEM((n, k_count // 2, TILE), f32),
            pltpu.VMEM((2, k_count // 2, TILE), f32),
            pltpu.VMEM((n, 2, k_count, block // 2), f32),
            pltpu.VMEM((2, k_count, block // 2), f32),
            pltpu.VMEM((2, k_count, block // 2), f32),
            pltpu.VMEM((k_count, block // 2), f32),
            pltpu.VMEM((k_count, block // 2), f32),
            pltpu.VMEM((k_count, block // 2), f32),
            pltpu.VMEM((n, k_count, width), f32),
            pltpu.VMEM((k_count, width), f32),
            pltpu.VMEM((k_count, width), f32),
            pltpu.VMEM((k_count, width), f32),
            pltpu.VMEM((k_count, width), f32),
            pltpu.SemaphoreType.DMA((len(PIECES),)),
            pltpu.SemaphoreType.DMA((5,)),
            pltpu.SemaphoreType.DMA((3, len(PIECES))),
            pltpu.SemaphoreType.DMA((3, len(PIECES))),
            pltpu.SemaphoreType.DMA((6, n)),
            pltpu.SemaphoreType.DMA((6, n)),
        ],
        compiler_params=pltpu.CompilerParams(
            collective_id=0, has_side_effects=True, vmem_limit_bytes=62 * 2**20
        ),
    )(
        genotype,
        allele_freq.reshape(1, -1),
        person_weight.reshape(-1, TILE),
        basis,
        residuals,
        block_markers.reshape(1, -1),
    )
    return pl.pallas_call(
        write_results,
        out_shape=shapes,
        in_specs=[vmem] * 4,
        out_specs=(hbm,) * 4,
        scratch_shapes=[pltpu.SemaphoreType.DMA((4,))],
    )(*[pltpu.with_memory_space_constraint(r, pltpu.VMEM) for r in results])


def solution(mesh):
    small = mesh.shape["people"] == 4 and mesh.shape["markers"] == 4
    placed = (
        P(("cohort", "people"), "markers"),
        P(("cohort", "markers")),
        P(("cohort", "people")),
        P("cohort", "markers"),
        P("cohort", "people"),
        P("markers"),
    )
    return jax.shard_map(
        fused if small else shards,
        mesh=mesh,
        in_specs=placed,
        out_specs=(
            P("cohort", "people"),
            P("cohort", None),
            P("markers", "cohort", "people"),
            P("markers", "cohort", "people"),
        ),
        check_vma=False,
    )
```

```python
import functools
import math

import jax
import jax.numpy as jnp
from jax import lax
from jax.experimental import pallas as pl
from jax.experimental.pallas import tpu as pltpu
from jax.sharding import PartitionSpec as P

MESH = pl.DeviceIdType.MESH


def from_partner(block, axis, apart):
    count = lax.axis_size(axis)
    route = []
    for low in range(count):
        high = low | 1 << apart
        if high != low and high < count:
            route += [(low, high), (high, low)]
    return lax.ppermute(block, axis, route)


def decode(packed, freq, weight):
    shifts = 2 * jnp.arange(4, dtype=jnp.int32)
    dosage = jnp.bitwise_and(jnp.right_shift(packed[:, :, None], shifts[None, None, :]), 3)
    dosage = dosage.reshape(packed.shape[0], packed.shape[1] * 4).astype(jnp.float32)
    standard = (dosage - 2.0 * freq[None, :]) / jnp.sqrt(2.0 * freq * (1.0 - freq))[None, :]
    return (weight[:, None] * standard).astype(jnp.bfloat16)


def shards(genotype, allele_freq, person_weight, basis, residuals, block_markers):
    weighted = decode(genotype, allele_freq, person_weight)
    rows_here = weighted.shape[0]
    marker_cols = weighted.shape[1]
    marker_count = lax.axis_size("markers")
    marker_index = lax.axis_index("markers")
    share_rows = rows_here // marker_count
    partial_value = lax.dot_general(
        basis, weighted, (((1,), (1,)), ((), ())), preferred_element_type=jnp.float32
    )
    full_sketch = lax.psum(partial_value, "markers")
    own_sketch = lax.dynamic_slice_in_dim(full_sketch, marker_index * share_rows, share_rows, 1)
    own_residual = lax.dynamic_slice_in_dim(
        residuals, marker_index * share_rows, share_rows, 1
    ).astype(jnp.float32)
    gram_local = jnp.dot(own_sketch, own_sketch.T, precision=lax.Precision.HIGHEST)
    factor_up = jnp.linalg.cholesky(gram_local).T
    levels = lax.axis_size(("people", "markers")).bit_length() - 1
    for level in range(levels):
        partner = from_partner(factor_up, ("people", "markers"), level)
        combined = jnp.dot(factor_up.T, factor_up, precision=lax.Precision.HIGHEST) + jnp.dot(
            partner.T, partner, precision=lax.Precision.HIGHEST
        )
        factor_up = jnp.linalg.cholesky(combined).T
    factor_low = factor_up.T
    ortho = jax.scipy.linalg.solve_triangular(factor_low, full_sketch, lower=True)
    ortho_share = lax.dynamic_slice_in_dim(ortho, marker_index * share_rows, share_rows, 1)
    coefficients = lax.psum(
        jnp.dot(ortho_share, own_residual.T, precision=lax.Precision.HIGHEST), ("people", "markers")
    )
    projected = (
        residuals.astype(jnp.float32)
        - jnp.dot(coefficients.T, ortho, precision=lax.Precision.HIGHEST)
    ).astype(jnp.bfloat16)
    ortho_half = ortho.astype(jnp.bfloat16)
    basis_partial = jnp.dot(ortho_half, weighted, preferred_element_type=jnp.float32)
    columns = block_markers - marker_index * marker_cols
    chosen = jnp.take(weighted, columns, axis=1)
    score_partial = jnp.dot(projected, chosen, preferred_element_type=jnp.float32)
    people_count = lax.axis_size("people")
    people_index = lax.axis_index("people")
    basis_total, score_total = lax.psum((basis_partial, score_partial), "people")
    basis_width = basis_total.shape[1] // people_count
    score_width = score_total.shape[1] // people_count
    basis_own = lax.dynamic_slice_in_dim(basis_total, people_index * basis_width, basis_width, 1)
    score_own = lax.dynamic_slice_in_dim(score_total, people_index * score_width, score_width, 1)
    total_people = rows_here * people_count
    root_people = math.sqrt(total_people)
    components = root_people * ortho
    scores = (score_own / root_people)[None]
    return (components, coefficients, basis_own[None], scores)


TILE = 128
PIECES = (512, 512, 512)


def split2(value):
    first = value.astype(jnp.bfloat16)
    second = (value - first.astype(jnp.float32)).astype(jnp.bfloat16)
    return jnp.concatenate([first, second], axis=0)


def split3(value):
    first = value.astype(jnp.bfloat16)
    left = value - first.astype(jnp.float32)
    second = left.astype(jnp.bfloat16)
    third = (left - second.astype(jnp.float32)).astype(jnp.bfloat16)
    return jnp.concatenate([first, second, third], axis=0)


def sum2(value):
    half = value.shape[0] // 2
    return value[:half] + value[half:]


def sum3(value):
    third = value.shape[0] // 3
    return value[:third] + value[third : 2 * third] + value[2 * third :]


def mm(left, right):
    return jnp.dot(left, right, preferred_element_type=jnp.float32)


def mm_nt(left, right):
    return lax.dot_general(
        left, right, (((1,), (1,)), ((), ())), preferred_element_type=jnp.float32
    )


def exact(left, right):
    return jnp.dot(
        left, right, preferred_element_type=jnp.float32, precision=lax.Precision.HIGHEST
    )


def eliminate(full, count):
    rows = lax.broadcasted_iota(jnp.int32, full.shape, 0)
    lanes = lax.broadcasted_iota(jnp.int32, full.shape, 1)
    for k in range(count):
        column = jnp.broadcast_to(full[:, k : k + 1], full.shape)
        row = full[k : k + 1, :] * (1.0 / column[k : k + 1, :])
        full = jnp.where(rows > k, full - column * row, full)
    pivots = jnp.sum(jnp.where(rows == lanes, full, 0.0), axis=1, keepdims=True)
    return full * (1.0 / jnp.sqrt(pivots))


def kernel(
    root_people,
    geno_hbm,
    freq_hbm,
    weight_hbm,
    basis_hbm,
    resid_hbm,
    block_hbm,
    comp_ref,
    coef_ref,
    next_ref,
    score_ref,
    geno,
    freq_ref,
    weight_ref,
    basis_ref,
    resid_ref,
    block_ref,
    dose,
    hot,
    perm,
    freq_rows,
    basis_rows,
    part,
    core_in,
    chip_part,
    chip_in,
    sketch_half,
    resid_score,
    resid_score_in,
    gram_part,
    gram_in,
    gram_sum,
    next_part,
    next_near,
    next_in,
    next_mine,
    next_pass,
    next_far,
    chosen_part,
    chosen_near,
    chosen_mine,
    chosen_pass,
    chosen_far,
    geno_sem,
    load_sem,
    pair_send,
    pair_recv,
    send_sem,
    recv_sem,
):
    people = lax.axis_index("people")
    markers = lax.axis_index("markers")
    n = 4
    half = part.shape[1]
    k_count = 2 * half
    block = dose.shape[2]
    words = block // 4
    core = lax.rem(markers, 2)
    core_peer = markers + 1 - 2 * core
    chip_peer = lax.rem(markers + 2, n)
    people_peer = [people, people + 1 - 2 * lax.rem(people, 2), lax.rem(people + 2, n), 3 - people]
    starts = [sum(PIECES[:i]) for i in range(len(PIECES))]
    spans = [pl.ds(start, size) for start, size in zip(starts, PIECES)]

    loads = []
    for i, span in enumerate(spans):
        loads.append(pltpu.make_async_copy(geno_hbm.at[span], geno.at[span], geno_sem.at[i]))
    small = [
        pltpu.make_async_copy(src, dst, load_sem.at[i])
        for i, (src, dst) in enumerate(
            (
                (freq_hbm, freq_ref),
                (basis_hbm, basis_ref),
                (weight_hbm, weight_ref),
                (block_hbm, block_ref),
                (resid_hbm, resid_ref),
            )
        )
    ]
    for load in small[:3] + loads + small[3:]:
        load.start()

    barrier = pltpu.get_barrier_semaphore()
    for peer in (core_peer, chip_peer):
        pl.semaphore_signal(barrier, inc=1, device_id={"markers": peer}, device_id_type=MESH)
    for d in (1, 2, 3):
        pl.semaphore_signal(
            barrier, inc=1, device_id={"people": people_peer[d]}, device_id_type=MESH
        )

    sends = {}

    def send(group, d, src, dst):
        copy = pltpu.make_async_remote_copy(
            src_ref=src,
            dst_ref=dst,
            send_sem=send_sem.at[len(sends)],
            recv_sem=recv_sem.at[len(sends)],
            device_id={"people": people_peer[d]} if d else {"markers": core_peer},
            device_id_type=MESH,
        )
        copy.start()
        sends[group, d] = copy

    pairs = {}

    def pair(level, i):
        src, dst, peer = (
            (part.at[1 - core], core_in, core_peer),
            (chip_part, chip_in, chip_peer),
            (sketch_half.at[core], sketch_half.at[core], core_peer),
        )[level]
        copy = pltpu.make_async_remote_copy(
            src_ref=src.at[:, spans[i]],
            dst_ref=dst.at[:, spans[i]],
            send_sem=pair_send.at[level, i],
            recv_sem=pair_recv.at[level, i],
            device_id={"markers": peer},
            device_id_type=MESH,
        )
        copy.start()
        pairs[level, i] = copy

    place = lax.broadcasted_iota(jnp.int32, (1, block), 1)
    source = 4 * lax.rem(place, words) + lax.div(place, words)
    marker = lax.broadcasted_iota(jnp.int32, (block, block), 0)
    perm[...] = jnp.where(marker == source, 1.0, 0.0).astype(jnp.bfloat16)
    small[0].wait()
    small[1].wait()
    small[2].wait()
    freq = jnp.concatenate([freq_ref[:, c * block : (c + 1) * block] for c in range(n)], axis=0)
    freq = jnp.concatenate([freq, freq], axis=0)
    freq = sum3(mm(split3(freq), perm[...]))[:n]
    twice = 2.0 * freq
    scale = 1.0 / jnp.sqrt(2.0 * freq * (1.0 - freq))
    freq_rows[0:n, :] = twice
    freq_rows[n : 2 * n, :] = scale
    basis = jnp.concatenate([basis_ref[:, c * block : (c + 1) * block] for c in range(n)], axis=0)
    basis = mm(basis, perm[...])
    offset = jnp.zeros((k_count, 1), jnp.float32)
    for c in range(n):
        scaled = (basis[c * k_count : (c + 1) * k_count] * scale[c : c + 1]).astype(jnp.bfloat16)
        basis_rows[c] = scaled
        offset += jnp.sum(
            scaled.astype(jnp.float32) * twice[c : c + 1], axis=1, keepdims=True
        )
    weight = jnp.concatenate(
        [weight_ref[i : i + 1, :] for i in range(weight_ref.shape[0])], axis=1
    )

    pl.semaphore_wait(barrier, 5)

    def forward(i):
        pairs[0, i].wait_recv()
        chip_part[:, spans[i]] = part[core, :, spans[i]] + core_in[:, spans[i]]
        pair(1, i)

    def finish(i):
        pairs[1, i].wait_recv()
        sketch_half[core, :, spans[i]] = chip_part[:, spans[i]] + chip_in[:, spans[i]]
        pair(2, i)

    for i, span in enumerate(spans):
        loads[i].wait()
        total = None
        for c in range(n):
            packed = geno[span, c * words : (c + 1) * words]
            tile = jnp.concatenate(
                [
                    jnp.bitwise_and(jnp.right_shift(packed, 2 * j), 3)
                    .astype(jnp.float32)
                    .astype(jnp.bfloat16)
                    for j in range(4)
                ],
                axis=1,
            )
            dose[c, span, :] = tile
            got = mm_nt(basis_rows[c], tile)
            total = got if total is None else total + got
        value = (total - offset) * weight[:, starts[i] : starts[i] + PIECES[i]]
        part[0, :, span] = value[:half]
        part[1, :, span] = value[half:]
        pair(0, i)
        if i:
            forward(i - 1)

    small[3].wait()
    small[4].wait()
    local = block_ref[...] - markers * (n * block)
    inner = lax.rem(local, block)
    column = lax.div(local, block) * block + lax.rem(inner, 4) * words + lax.div(inner, 4)
    for c in range(n):
        row = lax.broadcasted_iota(jnp.int32, (block, hot.shape[2]), 0) + c * block
        hot[c] = jnp.where(row == column, 1.0, 0.0).astype(jnp.bfloat16)
    forward(len(PIECES) - 1)

    def center(raw, sums, c):
        return (raw - sums * freq_rows[c : c + 1, :]) * freq_rows[n + c : n + c + 1, :]

    resid = resid_ref[...]
    heavy = split2(resid.astype(jnp.float32) * weight)
    sums = sum2(jnp.sum(heavy.astype(jnp.float32), axis=1, keepdims=True))
    picked = None
    for c in range(n):
        value = center(sum2(mm(heavy, dose[c])), sums, c)
        got = mm(split2(value), hot[c])
        picked = got if picked is None else picked + got
    picked = sum2(picked)
    width = picked.shape[1] // n
    for c in range(n):
        resid_score[c] = picked[:, c * width : (c + 1) * width]
    for d in (2, 3, 1):
        send(0, d, resid_score.at[people_peer[d]], resid_score_in.at[d - 1])

    for i in range(len(PIECES)):
        finish(i)
    for i in range(len(PIECES)):
        pairs[2, i].wait_recv()
    sketch = jnp.concatenate([sketch_half[0], sketch_half[1]], axis=0)
    heavy = split2(sketch * weight)
    sums = sum2(jnp.sum(heavy.astype(jnp.float32), axis=1, keepdims=True))
    cut = block // 2
    picked = None
    for d in (3, 2, 1, 0):
        c = people_peer[d]
        freq_row = freq_rows[pl.ds(c, 1), :]
        scale_row = freq_rows[pl.ds(c + n, 1), :]
        total = (sum2(mm(heavy, dose[c])) - sums * freq_row) * scale_row
        next_part[c, 0] = total[:, :cut]
        next_part[c, 1] = total[:, cut:]
        if d == 3:
            send(2, 1, next_part.at[c, 1], next_pass)
        if d > 1:
            send(2, d, next_part.at[c, 0], next_in.at[d - 2])
        got = mm(split2(total), hot[c])
        picked = got if picked is None else picked + got
        if d == 3:
            pieces = split3(sketch)
            gram = sum3(mm_nt(pieces, jnp.concatenate([pieces, resid], axis=0)))
            square = (
                gram[:, :k_count]
                + gram[:, k_count : 2 * k_count]
                + gram[:, 2 * k_count : 3 * k_count]
            )
            pad = jnp.zeros((k_count, k_count), jnp.float32)
            gram = jnp.concatenate([square, gram[:, 3 * k_count :], pad], axis=1)
            gram_part[0] = gram[:half]
            gram_part[1] = gram[half:]
            gram_in[people] = gram_part[core]
            for far in (3, 2, 1):
                send(1, far, gram_part.at[core], gram_in.at[people])
    picked = sum2(picked)
    for c in range(n):
        chosen_part[c] = picked[:, c * width : (c + 1) * width]
    send(4, 1, chosen_part.at[people_peer[3]], chosen_pass)
    send(5, 1, chosen_part.at[people_peer[1]], chosen_near)

    sends[2, 1].wait_recv()
    next_mine[...] = next_part[people_peer[2], 1] + next_pass[...]
    send(3, 2, next_mine, next_far)
    send(3, 1, next_part.at[people_peer[1]], next_near)
    for d in (1, 2, 3):
        sends[1, d].wait_recv()
    gram_sum[core] = gram_in[0] + gram_in[1] + gram_in[2] + gram_in[3]
    send(1, 0, gram_sum.at[core], gram_sum.at[core])
    sends[4, 1].wait_recv()
    chosen_mine[...] = chosen_part[people_peer[2]] + chosen_pass[...]
    send(4, 2, chosen_mine, chosen_far)
    sends[1, 0].wait_recv()
    full = jnp.concatenate([gram_sum[0], gram_sum[1]], axis=0)
    lane = lax.broadcasted_iota(jnp.int32, full.shape, 1)
    line = lax.broadcasted_iota(jnp.int32, full.shape, 0)
    full = jnp.where(lane == line + (TILE - k_count), 1.0, full)
    full = eliminate(full, k_count)
    coef = full[:, k_count : TILE - k_count]
    inverse = full[:, TILE - k_count :]
    coef_ref[...] = coef
    comp_ref[...] = root_people * exact(inverse, sketch)
    remover = lax.dot_general(
        coef,
        inverse,
        (((0,), (0,)), ((), ())),
        preferred_element_type=jnp.float32,
        precision=lax.Precision.HIGHEST,
    )

    for group, d in ((0, 1), (0, 2), (0, 3), (2, 2), (2, 3), (3, 1), (3, 2), (4, 2), (5, 1)):
        sends[group, d].wait_recv()
    total = next_part[people] + next_near[...]
    total = jnp.concatenate(
        [total[0] + next_in[0] + next_in[1], total[1] + next_far[...]], axis=1
    )
    chosen = chosen_part[people] + chosen_near[...] + chosen_far[...]
    scored = resid_score[people] + resid_score_in[0] + resid_score_in[1] + resid_score_in[2]
    solved = exact(inverse, total)
    next_ref[0] = sum3(mm_nt(split3(solved), perm[...]))
    score_ref[0] = (scored - exact(remover, chosen)) * (1.0 / root_people)
    for copy in list(pairs.values()) + list(sends.values()):
        copy.wait_send()


def write_results(*refs):
    sources, results, store_sem = refs[:4], refs[4:8], refs[8]
    stores = [pltpu.make_async_copy(sources[i], results[i], store_sem.at[i]) for i in range(4)]
    for store in stores:
        store.start()
    for store in stores:
        store.wait()


def fused(genotype, allele_freq, person_weight, basis, residuals, block_markers):
    n = 4
    rows, words = genotype.shape
    k_count = basis.shape[0]
    r_count = residuals.shape[0]
    block = 4 * words // n
    picks = block_markers.shape[0]
    width = picks // n
    f32, bf16 = jnp.float32, jnp.bfloat16
    hbm = pl.BlockSpec(memory_space=pltpu.HBM)
    vmem = pl.BlockSpec(memory_space=pltpu.VMEM)
    root_people = math.sqrt(rows * n)
    shapes = (
        jax.ShapeDtypeStruct((k_count, rows), f32),
        jax.ShapeDtypeStruct((k_count, r_count), f32),
        jax.ShapeDtypeStruct((1, k_count, block), f32),
        jax.ShapeDtypeStruct((1, r_count, width), f32),
    )
    results = pl.pallas_call(
        functools.partial(kernel, root_people),
        out_shape=tuple(pltpu.VMEM(shape.shape, shape.dtype) for shape in shapes),
        in_specs=[hbm] * 6,
        out_specs=(vmem,) * 4,
        scratch_shapes=[
            pltpu.VMEM((rows, words), jnp.int32),
            pltpu.VMEM((1, n * block), f32),
            pltpu.VMEM((rows // TILE, TILE), f32),
            pltpu.VMEM(basis.shape, bf16),
            pltpu.VMEM(residuals.shape, bf16),
            pltpu.VMEM((1, picks), jnp.int32),
            pltpu.VMEM((n, rows, block), bf16),
            pltpu.VMEM((n, block, picks), bf16),
            pltpu.VMEM((block, block), bf16),
            pltpu.VMEM((2 * n, block), f32),
            pltpu.VMEM((n, k_count, block), bf16),
            pltpu.VMEM((2, k_count // 2, rows), f32),
            pltpu.VMEM((k_count // 2, rows), f32),
            pltpu.VMEM((k_count // 2, rows), f32),
            pltpu.VMEM((k_count // 2, rows), f32),
            pltpu.VMEM((2, k_count // 2, rows), f32),
            pltpu.VMEM((n, r_count, width), f32),
            pltpu.VMEM((n - 1, r_count, width), f32),
            pltpu.VMEM((2, k_count // 2, TILE), f32),
            pltpu.VMEM((n, k_count // 2, TILE), f32),
            pltpu.VMEM((2, k_count // 2, TILE), f32),
            pltpu.VMEM((n, 2, k_count, block // 2), f32),
            pltpu.VMEM((2, k_count, block // 2), f32),
            pltpu.VMEM((2, k_count, block // 2), f32),
            pltpu.VMEM((k_count, block // 2), f32),
            pltpu.VMEM((k_count, block // 2), f32),
            pltpu.VMEM((k_count, block // 2), f32),
            pltpu.VMEM((n, k_count, width), f32),
            pltpu.VMEM((k_count, width), f32),
            pltpu.VMEM((k_count, width), f32),
            pltpu.VMEM((k_count, width), f32),
            pltpu.VMEM((k_count, width), f32),
            pltpu.SemaphoreType.DMA((len(PIECES),)),
            pltpu.SemaphoreType.DMA((5,)),
            pltpu.SemaphoreType.DMA((3, len(PIECES))),
            pltpu.SemaphoreType.DMA((3, len(PIECES))),
            pltpu.SemaphoreType.DMA((16,)),
            pltpu.SemaphoreType.DMA((16,)),
        ],
        compiler_params=pltpu.CompilerParams(
            collective_id=0, has_side_effects=True, vmem_limit_bytes=62 * 2**20
        ),
    )(
        genotype,
        allele_freq.reshape(1, -1),
        person_weight.reshape(-1, TILE),
        basis,
        residuals,
        block_markers.reshape(1, -1),
    )
    return pl.pallas_call(
        write_results,
        out_shape=shapes,
        in_specs=[vmem] * 4,
        out_specs=(hbm,) * 4,
        scratch_shapes=[pltpu.SemaphoreType.DMA((4,))],
    )(*[pltpu.with_memory_space_constraint(r, pltpu.VMEM) for r in results])


def solution(mesh):
    small = mesh.shape["people"] == 4 and mesh.shape["markers"] == 4
    placed = (
        P(("cohort", "people"), "markers"),
        P(("cohort", "markers")),
        P(("cohort", "people")),
        P("cohort", "markers"),
        P("cohort", "people"),
        P("markers"),
    )
    return jax.shard_map(
        fused if small else shards,
        mesh=mesh,
        in_specs=placed,
        out_specs=(
            P("cohort", "people"),
            P("cohort", None),
            P("markers", "cohort", "people"),
            P("markers", "cohort", "people"),
        ),
        check_vma=False,
    )
```

```python
import functools
import math

import jax
import jax.numpy as jnp
from jax import lax
from jax.experimental import pallas as pl
from jax.experimental.pallas import tpu as pltpu
from jax.sharding import PartitionSpec as P

MESH = pl.DeviceIdType.MESH


def from_partner(block, axis, apart):
    count = lax.axis_size(axis)
    route = []
    for low in range(count):
        high = low | 1 << apart
        if high != low and high < count:
            route += [(low, high), (high, low)]
    return lax.ppermute(block, axis, route)


def decode(packed, freq, weight):
    shifts = 2 * jnp.arange(4, dtype=jnp.int32)
    dosage = jnp.bitwise_and(jnp.right_shift(packed[:, :, None], shifts[None, None, :]), 3)
    dosage = dosage.reshape(packed.shape[0], packed.shape[1] * 4).astype(jnp.float32)
    standard = (dosage - 2.0 * freq[None, :]) / jnp.sqrt(2.0 * freq * (1.0 - freq))[None, :]
    return (weight[:, None] * standard).astype(jnp.bfloat16)


def shards(genotype, allele_freq, person_weight, basis, residuals, block_markers):
    weighted = decode(genotype, allele_freq, person_weight)
    rows_here = weighted.shape[0]
    marker_cols = weighted.shape[1]
    marker_count = lax.axis_size("markers")
    marker_index = lax.axis_index("markers")
    share_rows = rows_here // marker_count
    partial_value = lax.dot_general(
        basis, weighted, (((1,), (1,)), ((), ())), preferred_element_type=jnp.float32
    )
    full_sketch = lax.psum(partial_value, "markers")
    own_sketch = lax.dynamic_slice_in_dim(full_sketch, marker_index * share_rows, share_rows, 1)
    own_residual = lax.dynamic_slice_in_dim(
        residuals, marker_index * share_rows, share_rows, 1
    ).astype(jnp.float32)
    gram_local = jnp.dot(own_sketch, own_sketch.T, precision=lax.Precision.HIGHEST)
    factor_up = jnp.linalg.cholesky(gram_local).T
    levels = lax.axis_size(("people", "markers")).bit_length() - 1
    for level in range(levels):
        partner = from_partner(factor_up, ("people", "markers"), level)
        combined = jnp.dot(factor_up.T, factor_up, precision=lax.Precision.HIGHEST) + jnp.dot(
            partner.T, partner, precision=lax.Precision.HIGHEST
        )
        factor_up = jnp.linalg.cholesky(combined).T
    factor_low = factor_up.T
    ortho = jax.scipy.linalg.solve_triangular(factor_low, full_sketch, lower=True)
    ortho_share = lax.dynamic_slice_in_dim(ortho, marker_index * share_rows, share_rows, 1)
    coefficients = lax.psum(
        jnp.dot(ortho_share, own_residual.T, precision=lax.Precision.HIGHEST), ("people", "markers")
    )
    projected = (
        residuals.astype(jnp.float32)
        - jnp.dot(coefficients.T, ortho, precision=lax.Precision.HIGHEST)
    ).astype(jnp.bfloat16)
    ortho_half = ortho.astype(jnp.bfloat16)
    basis_partial = jnp.dot(ortho_half, weighted, preferred_element_type=jnp.float32)
    columns = block_markers - marker_index * marker_cols
    chosen = jnp.take(weighted, columns, axis=1)
    score_partial = jnp.dot(projected, chosen, preferred_element_type=jnp.float32)
    people_count = lax.axis_size("people")
    people_index = lax.axis_index("people")
    basis_total, score_total = lax.psum((basis_partial, score_partial), "people")
    basis_width = basis_total.shape[1] // people_count
    score_width = score_total.shape[1] // people_count
    basis_own = lax.dynamic_slice_in_dim(basis_total, people_index * basis_width, basis_width, 1)
    score_own = lax.dynamic_slice_in_dim(score_total, people_index * score_width, score_width, 1)
    total_people = rows_here * people_count
    root_people = math.sqrt(total_people)
    components = root_people * ortho
    scores = (score_own / root_people)[None]
    return (components, coefficients, basis_own[None], scores)


TILE = 128
PIECES = (512, 512, 512)


def split2(value):
    first = value.astype(jnp.bfloat16)
    second = (value - first.astype(jnp.float32)).astype(jnp.bfloat16)
    return jnp.concatenate([first, second], axis=0)


def split3(value):
    first = value.astype(jnp.bfloat16)
    left = value - first.astype(jnp.float32)
    second = left.astype(jnp.bfloat16)
    third = (left - second.astype(jnp.float32)).astype(jnp.bfloat16)
    return jnp.concatenate([first, second, third], axis=0)


def sum2(value):
    half = value.shape[0] // 2
    return value[:half] + value[half:]


def sum3(value):
    third = value.shape[0] // 3
    return value[:third] + value[third : 2 * third] + value[2 * third :]


def mm(left, right):
    return jnp.dot(left, right, preferred_element_type=jnp.float32)


def mm_nt(left, right):
    return lax.dot_general(
        left, right, (((1,), (1,)), ((), ())), preferred_element_type=jnp.float32
    )


def exact(left, right):
    return jnp.dot(
        left, right, preferred_element_type=jnp.float32, precision=lax.Precision.HIGHEST
    )


def thirds(value):
    pieces = split3(value)
    size = value.shape[0]
    return [pieces[i * size : (i + 1) * size] for i in range(3)]


def wide(value):
    first, second, third = thirds(value)
    return jnp.concatenate([first, first, second, first, second, third], axis=1)


def tall(value):
    first, second, third = thirds(value)
    return jnp.concatenate([first, second, first, third, second, first], axis=0)


def eliminate(full, count):
    rows = lax.broadcasted_iota(jnp.int32, full.shape, 0)
    lanes = lax.broadcasted_iota(jnp.int32, full.shape, 1)
    for k in range(count):
        column = jnp.broadcast_to(full[:, k : k + 1], full.shape)
        row = full[k : k + 1, :] * (1.0 / column[k : k + 1, :])
        full = jnp.where(rows > k, full - column * row, full)
    pivots = jnp.sum(jnp.where(rows == lanes, full, 0.0), axis=1, keepdims=True)
    return full * (1.0 / jnp.sqrt(pivots))


def kernel(
    root_people,
    geno_hbm,
    freq_hbm,
    weight_hbm,
    basis_hbm,
    resid_hbm,
    block_hbm,
    comp_ref,
    coef_ref,
    next_ref,
    score_ref,
    geno,
    freq_ref,
    weight_ref,
    basis_ref,
    resid_ref,
    block_ref,
    dose,
    hot,
    perm,
    freq_rows,
    basis_rows,
    part,
    core_in,
    chip_part,
    chip_in,
    sketch_half,
    resid_score,
    resid_score_in,
    gram_part,
    gram_in,
    gram_sum,
    next_part,
    next_near,
    next_in,
    next_mine,
    next_pass,
    next_far,
    chosen_part,
    chosen_near,
    chosen_mine,
    chosen_pass,
    chosen_far,
    sketch_tall,
    geno_sem,
    load_sem,
    pair_send,
    pair_recv,
    send_sem,
    recv_sem,
):
    people = lax.axis_index("people")
    markers = lax.axis_index("markers")
    n = 4
    half = part.shape[1]
    k_count = 2 * half
    block = dose.shape[2]
    words = block // 4
    core = lax.rem(markers, 2)
    core_peer = markers + 1 - 2 * core
    chip_peer = lax.rem(markers + 2, n)
    people_peer = [people, people + 1 - 2 * lax.rem(people, 2), lax.rem(people + 2, n), 3 - people]
    starts = [sum(PIECES[:i]) for i in range(len(PIECES))]
    spans = [pl.ds(start, size) for start, size in zip(starts, PIECES)]

    loads = []
    for i, span in enumerate(spans):
        loads.append(pltpu.make_async_copy(geno_hbm.at[span], geno.at[span], geno_sem.at[i]))
    small = [
        pltpu.make_async_copy(src, dst, load_sem.at[i])
        for i, (src, dst) in enumerate(
            (
                (freq_hbm, freq_ref),
                (basis_hbm, basis_ref),
                (weight_hbm, weight_ref),
                (block_hbm, block_ref),
                (resid_hbm, resid_ref),
            )
        )
    ]
    for load in small[:3] + loads + small[3:]:
        load.start()

    barrier = pltpu.get_barrier_semaphore()
    for peer in (core_peer, chip_peer):
        pl.semaphore_signal(barrier, inc=1, device_id={"markers": peer}, device_id_type=MESH)
    for d in (1, 2, 3):
        pl.semaphore_signal(
            barrier, inc=1, device_id={"people": people_peer[d]}, device_id_type=MESH
        )

    sends = {}

    def send(group, d, src, dst):
        copy = pltpu.make_async_remote_copy(
            src_ref=src,
            dst_ref=dst,
            send_sem=send_sem.at[len(sends)],
            recv_sem=recv_sem.at[len(sends)],
            device_id={"people": people_peer[d]} if d else {"markers": core_peer},
            device_id_type=MESH,
        )
        copy.start()
        sends[group, d] = copy

    pairs = {}

    def pair(level, i):
        src, dst, peer = (
            (part.at[1 - core], core_in, core_peer),
            (chip_part, chip_in, chip_peer),
            (sketch_half.at[core], sketch_half.at[core], core_peer),
        )[level]
        copy = pltpu.make_async_remote_copy(
            src_ref=src.at[:, spans[i]],
            dst_ref=dst.at[:, spans[i]],
            send_sem=pair_send.at[level, i],
            recv_sem=pair_recv.at[level, i],
            device_id={"markers": peer},
            device_id_type=MESH,
        )
        copy.start()
        pairs[level, i] = copy

    place = lax.broadcasted_iota(jnp.int32, (1, block), 1)
    source = 4 * lax.rem(place, words) + lax.div(place, words)
    marker = lax.broadcasted_iota(jnp.int32, (block, block), 0)
    perm[...] = jnp.where(marker == source, 1.0, 0.0).astype(jnp.bfloat16)
    small[0].wait()
    small[1].wait()
    small[2].wait()
    freq = jnp.concatenate([freq_ref[:, c * block : (c + 1) * block] for c in range(n)], axis=0)
    freq = jnp.concatenate([freq, freq], axis=0)
    freq = sum3(mm(split3(freq), perm[...]))[:n]
    twice = 2.0 * freq
    scale = 1.0 / jnp.sqrt(2.0 * freq * (1.0 - freq))
    freq_rows[0:n, :] = twice
    freq_rows[n : 2 * n, :] = scale
    basis = jnp.concatenate([basis_ref[:, c * block : (c + 1) * block] for c in range(n)], axis=0)
    basis = mm(basis, perm[...])
    offset = jnp.zeros((k_count, 1), jnp.float32)
    for c in range(n):
        scaled = (basis[c * k_count : (c + 1) * k_count] * scale[c : c + 1]).astype(jnp.bfloat16)
        basis_rows[c] = scaled
        offset += jnp.sum(
            scaled.astype(jnp.float32) * twice[c : c + 1], axis=1, keepdims=True
        )
    weight = jnp.concatenate(
        [weight_ref[i : i + 1, :] for i in range(weight_ref.shape[0])], axis=1
    )

    pl.semaphore_wait(barrier, 5)

    def forward(i):
        pairs[0, i].wait_recv()
        chip_part[:, spans[i]] = part[core, :, spans[i]] + core_in[:, spans[i]]
        pair(1, i)

    def finish(i):
        pairs[1, i].wait_recv()
        sketch_half[core, :, spans[i]] = chip_part[:, spans[i]] + chip_in[:, spans[i]]
        pair(2, i)

    for i, span in enumerate(spans):
        loads[i].wait()
        total = None
        for c in range(n):
            packed = geno[span, c * words : (c + 1) * words]
            tile = jnp.concatenate(
                [
                    jnp.bitwise_and(jnp.right_shift(packed, 2 * j), 3)
                    .astype(jnp.float32)
                    .astype(jnp.bfloat16)
                    for j in range(4)
                ],
                axis=1,
            )
            dose[c, span, :] = tile
            got = mm_nt(basis_rows[c], tile)
            total = got if total is None else total + got
        value = (total - offset) * weight[:, starts[i] : starts[i] + PIECES[i]]
        part[0, :, span] = value[:half]
        part[1, :, span] = value[half:]
        pair(0, i)
        if i:
            forward(i - 1)

    small[3].wait()
    small[4].wait()
    local = block_ref[...] - markers * (n * block)
    inner = lax.rem(local, block)
    column = lax.div(local, block) * block + lax.rem(inner, 4) * words + lax.div(inner, 4)
    for c in range(n):
        row = lax.broadcasted_iota(jnp.int32, (block, hot.shape[2]), 0) + c * block
        hot[c] = jnp.where(row == column, 1.0, 0.0).astype(jnp.bfloat16)
    forward(len(PIECES) - 1)

    def center(raw, sums, c):
        return (raw - sums * freq_rows[c : c + 1, :]) * freq_rows[n + c : n + c + 1, :]

    resid = resid_ref[...]
    heavy = split2(resid.astype(jnp.float32) * weight)
    sums = sum2(jnp.sum(heavy.astype(jnp.float32), axis=1, keepdims=True))
    picked = None
    for c in range(n):
        value = center(sum2(mm(heavy, dose[c])), sums, c)
        got = mm(split2(value), hot[c])
        picked = got if picked is None else picked + got
    picked = sum2(picked)
    width = picked.shape[1] // n
    for c in range(n):
        resid_score[c] = picked[:, c * width : (c + 1) * width]
    for d in (2, 3, 1):
        send(0, d, resid_score.at[people_peer[d]], resid_score_in.at[d - 1])

    for i in range(len(PIECES)):
        finish(i)
    for i in range(len(PIECES)):
        pairs[2, i].wait_recv()
    sketch = jnp.concatenate([sketch_half[0], sketch_half[1]], axis=0)
    heavy = split2(sketch * weight)
    sums = sum2(jnp.sum(heavy.astype(jnp.float32), axis=1, keepdims=True))
    cut = block // 2
    picked = None
    for d in (3, 2, 1, 0):
        c = people_peer[d]
        freq_row = freq_rows[pl.ds(c, 1), :]
        scale_row = freq_rows[pl.ds(c + n, 1), :]
        sides = [None, None]
        for side in (1, 0):
            at = slice(side * cut, (side + 1) * cut)
            raw = sum2(mm(heavy, dose[c, :, at]))
            sides[side] = (raw - sums * freq_row[:, at]) * scale_row[:, at]
            next_part[c, side] = sides[side]
            if d == 3 and side:
                send(2, 1, next_part.at[c, 1], next_pass)
                pieces = split3(sketch)
                gram = sum3(mm_nt(pieces, jnp.concatenate([pieces, resid], axis=0)))
                square = (
                    gram[:, :k_count]
                    + gram[:, k_count : 2 * k_count]
                    + gram[:, 2 * k_count : 3 * k_count]
                )
                pad = jnp.zeros((k_count, k_count), jnp.float32)
                gram = jnp.concatenate([square, gram[:, 3 * k_count :], pad], axis=1)
                gram_part[0] = gram[:half]
                gram_part[1] = gram[half:]
                gram_in[people] = gram_part[core]
                for far in (3, 2, 1):
                    send(1, far, gram_part.at[core], gram_in.at[people])
        total = jnp.concatenate(sides, axis=1)
        if d > 1:
            send(2, d, next_part.at[c, 0], next_in.at[d - 2])
        got = mm(split2(total), hot[c])
        picked = got if picked is None else picked + got
    picked = sum2(picked)
    for c in range(n):
        chosen_part[c] = picked[:, c * width : (c + 1) * width]
    send(4, 1, chosen_part.at[people_peer[3]], chosen_pass)
    send(5, 1, chosen_part.at[people_peer[1]], chosen_near)

    sketch_tall[...] = tall(sketch)
    sends[2, 1].wait_recv()
    next_mine[...] = next_part[people_peer[2], 1] + next_pass[...]
    send(3, 2, next_mine, next_far)
    send(3, 1, next_part.at[people_peer[1]], next_near)
    for d in (1, 2, 3):
        sends[1, d].wait_recv()
    gram_sum[core] = gram_in[0] + gram_in[1] + gram_in[2] + gram_in[3]
    send(1, 0, gram_sum.at[core], gram_sum.at[core])
    sends[4, 1].wait_recv()
    chosen_mine[...] = chosen_part[people_peer[2]] + chosen_pass[...]
    send(4, 2, chosen_mine, chosen_far)
    sends[1, 0].wait_recv()
    full = jnp.concatenate([gram_sum[0], gram_sum[1]], axis=0)
    lane = lax.broadcasted_iota(jnp.int32, full.shape, 1)
    line = lax.broadcasted_iota(jnp.int32, full.shape, 0)
    full = jnp.where(lane == line + (TILE - k_count), 1.0, full)
    full = eliminate(full, k_count)
    coef = full[:, k_count : TILE - k_count]
    inverse = full[:, TILE - k_count :]
    coef_ref[...] = coef
    left = wide(inverse)
    comp_ref[...] = root_people * mm(left, sketch_tall[...])
    remover = lax.dot_general(
        coef,
        inverse,
        (((0,), (0,)), ((), ())),
        preferred_element_type=jnp.float32,
        precision=lax.Precision.HIGHEST,
    )

    for group, d in ((0, 1), (0, 2), (0, 3), (2, 2), (2, 3), (3, 1), (3, 2), (4, 2), (5, 1)):
        sends[group, d].wait_recv()
    total = next_part[people] + next_near[...]
    total = jnp.concatenate(
        [total[0] + next_in[0] + next_in[1], total[1] + next_far[...]], axis=1
    )
    chosen = chosen_part[people] + chosen_near[...] + chosen_far[...]
    scored = resid_score[people] + resid_score_in[0] + resid_score_in[1] + resid_score_in[2]
    solved = mm(left, tall(total))
    next_ref[0] = sum2(mm_nt(split2(solved), perm[...]))
    score_ref[0] = (scored - exact(remover, chosen)) * (1.0 / root_people)
    for copy in list(pairs.values()) + list(sends.values()):
        copy.wait_send()


def write_results(*refs):
    sources, results, store_sem = refs[:4], refs[4:8], refs[8]
    stores = [pltpu.make_async_copy(sources[i], results[i], store_sem.at[i]) for i in range(4)]
    for store in stores:
        store.start()
    for store in stores:
        store.wait()


def fused(genotype, allele_freq, person_weight, basis, residuals, block_markers):
    n = 4
    rows, words = genotype.shape
    k_count = basis.shape[0]
    r_count = residuals.shape[0]
    block = 4 * words // n
    picks = block_markers.shape[0]
    width = picks // n
    f32, bf16 = jnp.float32, jnp.bfloat16
    hbm = pl.BlockSpec(memory_space=pltpu.HBM)
    vmem = pl.BlockSpec(memory_space=pltpu.VMEM)
    root_people = math.sqrt(rows * n)
    shapes = (
        jax.ShapeDtypeStruct((k_count, rows), f32),
        jax.ShapeDtypeStruct((k_count, r_count), f32),
        jax.ShapeDtypeStruct((1, k_count, block), f32),
        jax.ShapeDtypeStruct((1, r_count, width), f32),
    )
    results = pl.pallas_call(
        functools.partial(kernel, root_people),
        out_shape=tuple(pltpu.VMEM(shape.shape, shape.dtype) for shape in shapes),
        in_specs=[hbm] * 6,
        out_specs=(vmem,) * 4,
        scratch_shapes=[
            pltpu.VMEM((rows, words), jnp.int32),
            pltpu.VMEM((1, n * block), f32),
            pltpu.VMEM((rows // TILE, TILE), f32),
            pltpu.VMEM(basis.shape, bf16),
            pltpu.VMEM(residuals.shape, bf16),
            pltpu.VMEM((1, picks), jnp.int32),
            pltpu.VMEM((n, rows, block), bf16),
            pltpu.VMEM((n, block, picks), bf16),
            pltpu.VMEM((block, block), bf16),
            pltpu.VMEM((2 * n, block), f32),
            pltpu.VMEM((n, k_count, block), bf16),
            pltpu.VMEM((2, k_count // 2, rows), f32),
            pltpu.VMEM((k_count // 2, rows), f32),
            pltpu.VMEM((k_count // 2, rows), f32),
            pltpu.VMEM((k_count // 2, rows), f32),
            pltpu.VMEM((2, k_count // 2, rows), f32),
            pltpu.VMEM((n, r_count, width), f32),
            pltpu.VMEM((n - 1, r_count, width), f32),
            pltpu.VMEM((2, k_count // 2, TILE), f32),
            pltpu.VMEM((n, k_count // 2, TILE), f32),
            pltpu.VMEM((2, k_count // 2, TILE), f32),
            pltpu.VMEM((n, 2, k_count, block // 2), f32),
            pltpu.VMEM((2, k_count, block // 2), f32),
            pltpu.VMEM((2, k_count, block // 2), f32),
            pltpu.VMEM((k_count, block // 2), f32),
            pltpu.VMEM((k_count, block // 2), f32),
            pltpu.VMEM((k_count, block // 2), f32),
            pltpu.VMEM((n, k_count, width), f32),
            pltpu.VMEM((k_count, width), f32),
            pltpu.VMEM((k_count, width), f32),
            pltpu.VMEM((k_count, width), f32),
            pltpu.VMEM((k_count, width), f32),
            pltpu.VMEM((6 * k_count, rows), bf16),
            pltpu.SemaphoreType.DMA((len(PIECES),)),
            pltpu.SemaphoreType.DMA((5,)),
            pltpu.SemaphoreType.DMA((3, len(PIECES))),
            pltpu.SemaphoreType.DMA((3, len(PIECES))),
            pltpu.SemaphoreType.DMA((16,)),
            pltpu.SemaphoreType.DMA((16,)),
        ],
        compiler_params=pltpu.CompilerParams(
            collective_id=0, has_side_effects=True, vmem_limit_bytes=62 * 2**20
        ),
    )(
        genotype,
        allele_freq.reshape(1, -1),
        person_weight.reshape(-1, TILE),
        basis,
        residuals,
        block_markers.reshape(1, -1),
    )
    return pl.pallas_call(
        write_results,
        out_shape=shapes,
        in_specs=[vmem] * 4,
        out_specs=(hbm,) * 4,
        scratch_shapes=[pltpu.SemaphoreType.DMA((4,))],
    )(*[pltpu.with_memory_space_constraint(r, pltpu.VMEM) for r in results])


def solution(mesh):
    small = mesh.shape["people"] == 4 and mesh.shape["markers"] == 4
    placed = (
        P(("cohort", "people"), "markers"),
        P(("cohort", "markers")),
        P(("cohort", "people")),
        P("cohort", "markers"),
        P("cohort", "people"),
        P("markers"),
    )
    return jax.shard_map(
        fused if small else shards,
        mesh=mesh,
        in_specs=placed,
        out_specs=(
            P("cohort", "people"),
            P("cohort", None),
            P("markers", "cohort", "people"),
            P("markers", "cohort", "people"),
        ),
        check_vma=False,
    )
```

```python
import functools
import math

import jax
import jax.numpy as jnp
from jax import lax
from jax.experimental import pallas as pl
from jax.experimental.pallas import tpu as pltpu
from jax.sharding import PartitionSpec as P

MESH = pl.DeviceIdType.MESH


def from_partner(block, axis, apart):
    count = lax.axis_size(axis)
    route = []
    for low in range(count):
        high = low | 1 << apart
        if high != low and high < count:
            route += [(low, high), (high, low)]
    return lax.ppermute(block, axis, route)


def decode(packed, freq, weight):
    shifts = 2 * jnp.arange(4, dtype=jnp.int32)
    dosage = jnp.bitwise_and(jnp.right_shift(packed[:, :, None], shifts[None, None, :]), 3)
    dosage = dosage.reshape(packed.shape[0], packed.shape[1] * 4).astype(jnp.float32)
    standard = (dosage - 2.0 * freq[None, :]) / jnp.sqrt(2.0 * freq * (1.0 - freq))[None, :]
    return (weight[:, None] * standard).astype(jnp.bfloat16)


def shards(genotype, allele_freq, person_weight, basis, residuals, block_markers):
    weighted = decode(genotype, allele_freq, person_weight)
    rows_here = weighted.shape[0]
    marker_cols = weighted.shape[1]
    marker_count = lax.axis_size("markers")
    marker_index = lax.axis_index("markers")
    share_rows = rows_here // marker_count
    partial_value = lax.dot_general(
        basis, weighted, (((1,), (1,)), ((), ())), preferred_element_type=jnp.float32
    )
    full_sketch = lax.psum(partial_value, "markers")
    own_sketch = lax.dynamic_slice_in_dim(full_sketch, marker_index * share_rows, share_rows, 1)
    own_residual = lax.dynamic_slice_in_dim(
        residuals, marker_index * share_rows, share_rows, 1
    ).astype(jnp.float32)
    gram_local = jnp.dot(own_sketch, own_sketch.T, precision=lax.Precision.HIGHEST)
    factor_up = jnp.linalg.cholesky(gram_local).T
    levels = lax.axis_size(("people", "markers")).bit_length() - 1
    for level in range(levels):
        partner = from_partner(factor_up, ("people", "markers"), level)
        combined = jnp.dot(factor_up.T, factor_up, precision=lax.Precision.HIGHEST) + jnp.dot(
            partner.T, partner, precision=lax.Precision.HIGHEST
        )
        factor_up = jnp.linalg.cholesky(combined).T
    factor_low = factor_up.T
    ortho = jax.scipy.linalg.solve_triangular(factor_low, full_sketch, lower=True)
    ortho_share = lax.dynamic_slice_in_dim(ortho, marker_index * share_rows, share_rows, 1)
    coefficients = lax.psum(
        jnp.dot(ortho_share, own_residual.T, precision=lax.Precision.HIGHEST), ("people", "markers")
    )
    projected = (
        residuals.astype(jnp.float32)
        - jnp.dot(coefficients.T, ortho, precision=lax.Precision.HIGHEST)
    ).astype(jnp.bfloat16)
    ortho_half = ortho.astype(jnp.bfloat16)
    basis_partial = jnp.dot(ortho_half, weighted, preferred_element_type=jnp.float32)
    columns = block_markers - marker_index * marker_cols
    chosen = jnp.take(weighted, columns, axis=1)
    score_partial = jnp.dot(projected, chosen, preferred_element_type=jnp.float32)
    people_count = lax.axis_size("people")
    people_index = lax.axis_index("people")
    basis_total, score_total = lax.psum((basis_partial, score_partial), "people")
    basis_width = basis_total.shape[1] // people_count
    score_width = score_total.shape[1] // people_count
    basis_own = lax.dynamic_slice_in_dim(basis_total, people_index * basis_width, basis_width, 1)
    score_own = lax.dynamic_slice_in_dim(score_total, people_index * score_width, score_width, 1)
    total_people = rows_here * people_count
    root_people = math.sqrt(total_people)
    components = root_people * ortho
    scores = (score_own / root_people)[None]
    return (components, coefficients, basis_own[None], scores)


TILE = 128
PIECES = (512, 512, 512)


def split2(value):
    first = value.astype(jnp.bfloat16)
    second = (value - first.astype(jnp.float32)).astype(jnp.bfloat16)
    return jnp.concatenate([first, second], axis=0)


def split3(value):
    first = value.astype(jnp.bfloat16)
    left = value - first.astype(jnp.float32)
    second = left.astype(jnp.bfloat16)
    third = (left - second.astype(jnp.float32)).astype(jnp.bfloat16)
    return jnp.concatenate([first, second, third], axis=0)


def sum2(value):
    half = value.shape[0] // 2
    return value[:half] + value[half:]


def sum3(value):
    third = value.shape[0] // 3
    return value[:third] + value[third : 2 * third] + value[2 * third :]


def mm(left, right):
    return jnp.dot(left, right, preferred_element_type=jnp.float32)


def mm_nt(left, right):
    return lax.dot_general(
        left, right, (((1,), (1,)), ((), ())), preferred_element_type=jnp.float32
    )


def exact(left, right):
    return jnp.dot(
        left, right, preferred_element_type=jnp.float32, precision=lax.Precision.HIGHEST
    )


def thirds(value):
    pieces = split3(value)
    size = value.shape[0]
    return [pieces[i * size : (i + 1) * size] for i in range(3)]


def wide(value):
    first, second, third = thirds(value)
    return jnp.concatenate([first, first, second, first, second, third], axis=1)


def tall(value):
    first, second, third = thirds(value)
    return jnp.concatenate([first, second, first, third, second, first], axis=0)


def eliminate(full, count):
    rows = lax.broadcasted_iota(jnp.int32, full.shape, 0)
    lanes = lax.broadcasted_iota(jnp.int32, full.shape, 1)
    for k in range(count):
        column = jnp.broadcast_to(full[:, k : k + 1], full.shape)
        row = full[k : k + 1, :] * (1.0 / column[k : k + 1, :])
        full = jnp.where(rows > k, full - column * row, full)
    pivots = jnp.sum(jnp.where(rows == lanes, full, 0.0), axis=1, keepdims=True)
    return full * (1.0 / jnp.sqrt(pivots))


def kernel(
    root_people,
    geno_hbm,
    freq_hbm,
    weight_hbm,
    basis_hbm,
    resid_hbm,
    block_hbm,
    comp_ref,
    coef_ref,
    next_ref,
    score_ref,
    geno,
    freq_ref,
    weight_ref,
    basis_ref,
    resid_ref,
    block_ref,
    dose,
    hot,
    perm,
    freq_rows,
    basis_rows,
    part,
    core_in,
    chip_part,
    chip_in,
    sketch_half,
    resid_score,
    resid_score_in,
    gram_part,
    gram_in,
    gram_sum,
    next_part,
    next_near,
    next_in,
    next_mine,
    next_pass,
    next_far,
    chosen_part,
    chosen_near,
    chosen_mine,
    chosen_pass,
    chosen_far,
    sketch_tall,
    geno_sem,
    load_sem,
    pair_send,
    pair_recv,
    send_sem,
    recv_sem,
):
    people = lax.axis_index("people")
    markers = lax.axis_index("markers")
    n = 4
    half = part.shape[1]
    k_count = 2 * half
    block = dose.shape[2]
    words = block // 4
    core = lax.rem(markers, 2)
    core_peer = markers + 1 - 2 * core
    chip_peer = lax.rem(markers + 2, n)
    people_peer = [people, people + 1 - 2 * lax.rem(people, 2), lax.rem(people + 2, n), 3 - people]
    starts = [sum(PIECES[:i]) for i in range(len(PIECES))]
    spans = [pl.ds(start, size) for start, size in zip(starts, PIECES)]

    loads = []
    for i, span in enumerate(spans):
        loads.append(pltpu.make_async_copy(geno_hbm.at[span], geno.at[span], geno_sem.at[i]))
    small = [
        pltpu.make_async_copy(src, dst, load_sem.at[i])
        for i, (src, dst) in enumerate(
            (
                (freq_hbm, freq_ref),
                (basis_hbm, basis_ref),
                (weight_hbm, weight_ref),
                (block_hbm, block_ref),
                (resid_hbm, resid_ref),
            )
        )
    ]
    for load in small[:3] + loads + small[3:]:
        load.start()

    barrier = pltpu.get_barrier_semaphore()
    for peer in (core_peer, chip_peer):
        pl.semaphore_signal(barrier, inc=1, device_id={"markers": peer}, device_id_type=MESH)
    for d in (1, 2, 3):
        pl.semaphore_signal(
            barrier, inc=1, device_id={"people": people_peer[d]}, device_id_type=MESH
        )

    sends = {}

    def send(group, d, src, dst):
        copy = pltpu.make_async_remote_copy(
            src_ref=src,
            dst_ref=dst,
            send_sem=send_sem.at[len(sends)],
            recv_sem=recv_sem.at[len(sends)],
            device_id={"people": people_peer[d]} if d else {"markers": core_peer},
            device_id_type=MESH,
        )
        copy.start()
        sends[group, d] = copy

    pairs = {}

    def pair(level, i):
        src, dst, peer = (
            (part.at[1 - core], core_in, core_peer),
            (chip_part, chip_in, chip_peer),
            (sketch_half.at[core], sketch_half.at[core], core_peer),
        )[level]
        copy = pltpu.make_async_remote_copy(
            src_ref=src.at[:, spans[i]],
            dst_ref=dst.at[:, spans[i]],
            send_sem=pair_send.at[level, i],
            recv_sem=pair_recv.at[level, i],
            device_id={"markers": peer},
            device_id_type=MESH,
        )
        copy.start()
        pairs[level, i] = copy

    place = lax.broadcasted_iota(jnp.int32, (1, block), 1)
    source = 4 * lax.rem(place, words) + lax.div(place, words)
    marker = lax.broadcasted_iota(jnp.int32, (block, block), 0)
    perm[...] = jnp.where(marker == source, 1.0, 0.0).astype(jnp.bfloat16)
    small[0].wait()
    small[1].wait()
    small[2].wait()
    freq = jnp.concatenate([freq_ref[:, c * block : (c + 1) * block] for c in range(n)], axis=0)
    freq = jnp.concatenate([freq, freq], axis=0)
    freq = sum3(mm(split3(freq), perm[...]))[:n]
    twice = 2.0 * freq
    scale = 1.0 / jnp.sqrt(2.0 * freq * (1.0 - freq))
    freq_rows[0:n, :] = twice
    freq_rows[n : 2 * n, :] = scale
    basis = jnp.concatenate([basis_ref[:, c * block : (c + 1) * block] for c in range(n)], axis=0)
    basis = mm(basis, perm[...])
    offset = jnp.zeros((k_count, 1), jnp.float32)
    for c in range(n):
        scaled = (basis[c * k_count : (c + 1) * k_count] * scale[c : c + 1]).astype(jnp.bfloat16)
        basis_rows[c] = scaled
        offset += jnp.sum(
            scaled.astype(jnp.float32) * twice[c : c + 1], axis=1, keepdims=True
        )
    weight = jnp.concatenate(
        [weight_ref[i : i + 1, :] for i in range(weight_ref.shape[0])], axis=1
    )

    def forward(i):
        pairs[0, i].wait_recv()
        chip_part[:, spans[i]] = part[core, :, spans[i]] + core_in[:, spans[i]]
        pair(1, i)

    def finish(i):
        pairs[1, i].wait_recv()
        sketch_half[core, :, spans[i]] = chip_part[:, spans[i]] + chip_in[:, spans[i]]
        pair(2, i)

    for i, span in enumerate(spans):
        loads[i].wait()
        total = None
        for c in range(n):
            packed = geno[span, c * words : (c + 1) * words]
            digits = [
                jnp.bitwise_and(packed, 3),
                jnp.bitwise_and(jnp.right_shift(packed, 2), 3),
                jnp.bitwise_and(jnp.right_shift(packed, 4), 3),
                jnp.right_shift(packed, 6),
            ]
            tile = jnp.concatenate(
                [digit.astype(jnp.float32).astype(jnp.bfloat16) for digit in digits], axis=1
            )
            dose[c, span, :] = tile
            got = mm_nt(basis_rows[c], tile)
            total = got if total is None else total + got
        value = (total - offset) * weight[:, starts[i] : starts[i] + PIECES[i]]
        part[0, :, span] = value[:half]
        part[1, :, span] = value[half:]
        if i == 0:
            pl.semaphore_wait(barrier, 5)
        pair(0, i)
        if i:
            forward(i - 1)

    small[3].wait()
    small[4].wait()
    local = block_ref[...] - markers * (n * block)
    inner = lax.rem(local, block)
    column = lax.div(local, block) * block + lax.rem(inner, 4) * words + lax.div(inner, 4)
    for c in range(n):
        row = lax.broadcasted_iota(jnp.int32, (block, hot.shape[2]), 0) + c * block
        hot[c] = jnp.where(row == column, 1.0, 0.0).astype(jnp.bfloat16)
    forward(len(PIECES) - 1)

    def center(raw, sums, c):
        return (raw - sums * freq_rows[c : c + 1, :]) * freq_rows[n + c : n + c + 1, :]

    resid = resid_ref[...]
    heavy = split2(resid.astype(jnp.float32) * weight)
    sums = sum2(jnp.sum(heavy.astype(jnp.float32), axis=1, keepdims=True))
    picked = None
    for c in range(n):
        value = center(sum2(mm(heavy, dose[c])), sums, c)
        got = mm(split2(value), hot[c])
        picked = got if picked is None else picked + got
    picked = sum2(picked)
    width = picked.shape[1] // n
    for c in range(n):
        resid_score[c] = picked[:, c * width : (c + 1) * width]
    for d in (2, 3, 1):
        send(0, d, resid_score.at[people_peer[d]], resid_score_in.at[d - 1])

    for i in range(len(PIECES)):
        finish(i)
    for i in range(len(PIECES)):
        pairs[2, i].wait_recv()
    sketch = jnp.concatenate([sketch_half[0], sketch_half[1]], axis=0)
    heavy = split2(sketch * weight)
    sums = sum2(jnp.sum(heavy.astype(jnp.float32), axis=1, keepdims=True))
    cut = block // 2
    picked = None
    for d in (3, 2, 1, 0):
        c = people_peer[d]
        freq_row = freq_rows[pl.ds(c, 1), :]
        scale_row = freq_rows[pl.ds(c + n, 1), :]
        sides = [None, None]
        for side in (1, 0):
            at = slice(side * cut, (side + 1) * cut)
            raw = sum2(mm(heavy, dose[c, :, at]))
            sides[side] = (raw - sums * freq_row[:, at]) * scale_row[:, at]
            next_part[c, side] = sides[side]
            if d == 3 and side:
                send(2, 1, next_part.at[c, 1], next_pass)
                pieces = split3(sketch)
                gram = sum3(mm_nt(pieces, jnp.concatenate([pieces, resid], axis=0)))
                square = (
                    gram[:, :k_count]
                    + gram[:, k_count : 2 * k_count]
                    + gram[:, 2 * k_count : 3 * k_count]
                )
                pad = jnp.zeros((k_count, k_count), jnp.float32)
                gram = jnp.concatenate([square, gram[:, 3 * k_count :], pad], axis=1)
                gram_part[0] = gram[:half]
                gram_part[1] = gram[half:]
                gram_in[people] = gram_part[core]
                for far in (3, 2, 1):
                    send(1, far, gram_part.at[core], gram_in.at[people])
        total = jnp.concatenate(sides, axis=1)
        if d > 1:
            send(2, d, next_part.at[c, 0], next_in.at[d - 2])
        got = mm(split2(total), hot[c])
        picked = got if picked is None else picked + got
    picked = sum2(picked)
    for c in range(n):
        chosen_part[c] = picked[:, c * width : (c + 1) * width]
    send(4, 1, chosen_part.at[people_peer[3]], chosen_pass)
    send(5, 1, chosen_part.at[people_peer[1]], chosen_near)

    sketch_tall[...] = tall(sketch)
    sends[2, 1].wait_recv()
    next_mine[...] = next_part[people_peer[2], 1] + next_pass[...]
    send(3, 2, next_mine, next_far)
    send(3, 1, next_part.at[people_peer[1]], next_near)
    for d in (1, 2, 3):
        sends[1, d].wait_recv()
    gram_sum[core] = gram_in[0] + gram_in[1] + gram_in[2] + gram_in[3]
    send(1, 0, gram_sum.at[core], gram_sum.at[core])
    sends[4, 1].wait_recv()
    chosen_mine[...] = chosen_part[people_peer[2]] + chosen_pass[...]
    send(4, 2, chosen_mine, chosen_far)
    sends[1, 0].wait_recv()
    full = jnp.concatenate([gram_sum[0], gram_sum[1]], axis=0)
    lane = lax.broadcasted_iota(jnp.int32, full.shape, 1)
    line = lax.broadcasted_iota(jnp.int32, full.shape, 0)
    full = jnp.where(lane == line + (TILE - k_count), 1.0, full)
    full = eliminate(full, k_count)
    coef = full[:, k_count : TILE - k_count]
    inverse = full[:, TILE - k_count :]
    coef_ref[...] = coef
    left = wide(inverse)
    comp_ref[...] = root_people * mm(left, sketch_tall[...])
    remover = lax.dot_general(
        coef,
        inverse,
        (((0,), (0,)), ((), ())),
        preferred_element_type=jnp.float32,
        precision=lax.Precision.HIGHEST,
    )

    for group, d in ((0, 1), (0, 2), (0, 3), (2, 2), (2, 3), (3, 1), (3, 2), (4, 2), (5, 1)):
        sends[group, d].wait_recv()
    total = next_part[people] + next_near[...]
    total = jnp.concatenate(
        [total[0] + next_in[0] + next_in[1], total[1] + next_far[...]], axis=1
    )
    chosen = chosen_part[people] + chosen_near[...] + chosen_far[...]
    scored = resid_score[people] + resid_score_in[0] + resid_score_in[1] + resid_score_in[2]
    solved = mm(left, tall(total))
    next_ref[0] = sum2(mm_nt(split2(solved), perm[...]))
    score_ref[0] = (scored - exact(remover, chosen)) * (1.0 / root_people)
    for copy in list(pairs.values()) + list(sends.values()):
        copy.wait_send()


def write_results(*refs):
    sources, results, store_sem = refs[:4], refs[4:8], refs[8]
    stores = [pltpu.make_async_copy(sources[i], results[i], store_sem.at[i]) for i in range(4)]
    for store in stores:
        store.start()
    for store in stores:
        store.wait()


def fused(genotype, allele_freq, person_weight, basis, residuals, block_markers):
    n = 4
    rows, words = genotype.shape
    k_count = basis.shape[0]
    r_count = residuals.shape[0]
    block = 4 * words // n
    picks = block_markers.shape[0]
    width = picks // n
    f32, bf16 = jnp.float32, jnp.bfloat16
    hbm = pl.BlockSpec(memory_space=pltpu.HBM)
    vmem = pl.BlockSpec(memory_space=pltpu.VMEM)
    root_people = math.sqrt(rows * n)
    shapes = (
        jax.ShapeDtypeStruct((k_count, rows), f32),
        jax.ShapeDtypeStruct((k_count, r_count), f32),
        jax.ShapeDtypeStruct((1, k_count, block), f32),
        jax.ShapeDtypeStruct((1, r_count, width), f32),
    )
    results = pl.pallas_call(
        functools.partial(kernel, root_people),
        out_shape=tuple(pltpu.VMEM(shape.shape, shape.dtype) for shape in shapes),
        in_specs=[hbm] * 6,
        out_specs=(vmem,) * 4,
        scratch_shapes=[
            pltpu.VMEM((rows, words), jnp.int32),
            pltpu.VMEM((1, n * block), f32),
            pltpu.VMEM((rows // TILE, TILE), f32),
            pltpu.VMEM(basis.shape, bf16),
            pltpu.VMEM(residuals.shape, bf16),
            pltpu.VMEM((1, picks), jnp.int32),
            pltpu.VMEM((n, rows, block), bf16),
            pltpu.VMEM((n, block, picks), bf16),
            pltpu.VMEM((block, block), bf16),
            pltpu.VMEM((2 * n, block), f32),
            pltpu.VMEM((n, k_count, block), bf16),
            pltpu.VMEM((2, k_count // 2, rows), f32),
            pltpu.VMEM((k_count // 2, rows), f32),
            pltpu.VMEM((k_count // 2, rows), f32),
            pltpu.VMEM((k_count // 2, rows), f32),
            pltpu.VMEM((2, k_count // 2, rows), f32),
            pltpu.VMEM((n, r_count, width), f32),
            pltpu.VMEM((n - 1, r_count, width), f32),
            pltpu.VMEM((2, k_count // 2, TILE), f32),
            pltpu.VMEM((n, k_count // 2, TILE), f32),
            pltpu.VMEM((2, k_count // 2, TILE), f32),
            pltpu.VMEM((n, 2, k_count, block // 2), f32),
            pltpu.VMEM((2, k_count, block // 2), f32),
            pltpu.VMEM((2, k_count, block // 2), f32),
            pltpu.VMEM((k_count, block // 2), f32),
            pltpu.VMEM((k_count, block // 2), f32),
            pltpu.VMEM((k_count, block // 2), f32),
            pltpu.VMEM((n, k_count, width), f32),
            pltpu.VMEM((k_count, width), f32),
            pltpu.VMEM((k_count, width), f32),
            pltpu.VMEM((k_count, width), f32),
            pltpu.VMEM((k_count, width), f32),
            pltpu.VMEM((6 * k_count, rows), bf16),
            pltpu.SemaphoreType.DMA((len(PIECES),)),
            pltpu.SemaphoreType.DMA((5,)),
            pltpu.SemaphoreType.DMA((3, len(PIECES))),
            pltpu.SemaphoreType.DMA((3, len(PIECES))),
            pltpu.SemaphoreType.DMA((16,)),
            pltpu.SemaphoreType.DMA((16,)),
        ],
        compiler_params=pltpu.CompilerParams(
            collective_id=0, has_side_effects=True, vmem_limit_bytes=62 * 2**20
        ),
    )(
        genotype,
        allele_freq.reshape(1, -1),
        person_weight.reshape(-1, TILE),
        basis,
        residuals,
        block_markers.reshape(1, -1),
    )
    return pl.pallas_call(
        write_results,
        out_shape=shapes,
        in_specs=[vmem] * 4,
        out_specs=(hbm,) * 4,
        scratch_shapes=[pltpu.SemaphoreType.DMA((4,))],
    )(*[pltpu.with_memory_space_constraint(r, pltpu.VMEM) for r in results])


def solution(mesh):
    small = mesh.shape["people"] == 4 and mesh.shape["markers"] == 4
    placed = (
        P(("cohort", "people"), "markers"),
        P(("cohort", "markers")),
        P(("cohort", "people")),
        P("cohort", "markers"),
        P("cohort", "people"),
        P("markers"),
    )
    return jax.shard_map(
        fused if small else shards,
        mesh=mesh,
        in_specs=placed,
        out_specs=(
            P("cohort", "people"),
            P("cohort", None),
            P("markers", "cohort", "people"),
            P("markers", "cohort", "people"),
        ),
        check_vma=False,
    )
```

```python
import functools
import math

import jax
import jax.numpy as jnp
from jax import lax
from jax.experimental import pallas as pl
from jax.experimental.pallas import tpu as pltpu
from jax.sharding import PartitionSpec as P

MESH = pl.DeviceIdType.MESH


def from_partner(block, axis, apart):
    count = lax.axis_size(axis)
    route = []
    for low in range(count):
        high = low | 1 << apart
        if high != low and high < count:
            route += [(low, high), (high, low)]
    return lax.ppermute(block, axis, route)


def decode(packed, freq, weight):
    shifts = 2 * jnp.arange(4, dtype=jnp.int32)
    dosage = jnp.bitwise_and(jnp.right_shift(packed[:, :, None], shifts[None, None, :]), 3)
    dosage = dosage.reshape(packed.shape[0], packed.shape[1] * 4).astype(jnp.float32)
    standard = (dosage - 2.0 * freq[None, :]) / jnp.sqrt(2.0 * freq * (1.0 - freq))[None, :]
    return (weight[:, None] * standard).astype(jnp.bfloat16)


def shards(genotype, allele_freq, person_weight, basis, residuals, block_markers):
    weighted = decode(genotype, allele_freq, person_weight)
    rows_here = weighted.shape[0]
    marker_cols = weighted.shape[1]
    marker_count = lax.axis_size("markers")
    marker_index = lax.axis_index("markers")
    share_rows = rows_here // marker_count
    partial_value = lax.dot_general(
        basis, weighted, (((1,), (1,)), ((), ())), preferred_element_type=jnp.float32
    )
    full_sketch = lax.psum(partial_value, "markers")
    own_sketch = lax.dynamic_slice_in_dim(full_sketch, marker_index * share_rows, share_rows, 1)
    own_residual = lax.dynamic_slice_in_dim(
        residuals, marker_index * share_rows, share_rows, 1
    ).astype(jnp.float32)
    gram_local = jnp.dot(own_sketch, own_sketch.T, precision=lax.Precision.HIGHEST)
    factor_up = jnp.linalg.cholesky(gram_local).T
    levels = lax.axis_size(("people", "markers")).bit_length() - 1
    for level in range(levels):
        partner = from_partner(factor_up, ("people", "markers"), level)
        combined = jnp.dot(factor_up.T, factor_up, precision=lax.Precision.HIGHEST) + jnp.dot(
            partner.T, partner, precision=lax.Precision.HIGHEST
        )
        factor_up = jnp.linalg.cholesky(combined).T
    factor_low = factor_up.T
    ortho = jax.scipy.linalg.solve_triangular(factor_low, full_sketch, lower=True)
    ortho_share = lax.dynamic_slice_in_dim(ortho, marker_index * share_rows, share_rows, 1)
    coefficients = lax.psum(
        jnp.dot(ortho_share, own_residual.T, precision=lax.Precision.HIGHEST), ("people", "markers")
    )
    projected = (
        residuals.astype(jnp.float32)
        - jnp.dot(coefficients.T, ortho, precision=lax.Precision.HIGHEST)
    ).astype(jnp.bfloat16)
    ortho_half = ortho.astype(jnp.bfloat16)
    basis_partial = jnp.dot(ortho_half, weighted, preferred_element_type=jnp.float32)
    columns = block_markers - marker_index * marker_cols
    chosen = jnp.take(weighted, columns, axis=1)
    score_partial = jnp.dot(projected, chosen, preferred_element_type=jnp.float32)
    people_count = lax.axis_size("people")
    people_index = lax.axis_index("people")
    basis_total, score_total = lax.psum((basis_partial, score_partial), "people")
    basis_width = basis_total.shape[1] // people_count
    score_width = score_total.shape[1] // people_count
    basis_own = lax.dynamic_slice_in_dim(basis_total, people_index * basis_width, basis_width, 1)
    score_own = lax.dynamic_slice_in_dim(score_total, people_index * score_width, score_width, 1)
    total_people = rows_here * people_count
    root_people = math.sqrt(total_people)
    components = root_people * ortho
    scores = (score_own / root_people)[None]
    return (components, coefficients, basis_own[None], scores)


TILE = 128
PIECES = (512, 512, 512)


def split2(value):
    first = value.astype(jnp.bfloat16)
    second = (value - first.astype(jnp.float32)).astype(jnp.bfloat16)
    return jnp.concatenate([first, second], axis=0)


def split3(value):
    first = value.astype(jnp.bfloat16)
    left = value - first.astype(jnp.float32)
    second = left.astype(jnp.bfloat16)
    third = (left - second.astype(jnp.float32)).astype(jnp.bfloat16)
    return jnp.concatenate([first, second, third], axis=0)


def sum2(value):
    half = value.shape[0] // 2
    return value[:half] + value[half:]


def sum3(value):
    third = value.shape[0] // 3
    return value[:third] + value[third : 2 * third] + value[2 * third :]


def mm(left, right):
    return jnp.dot(left, right, preferred_element_type=jnp.float32)


def mm_nt(left, right):
    return lax.dot_general(
        left, right, (((1,), (1,)), ((), ())), preferred_element_type=jnp.float32
    )


def exact(left, right):
    return jnp.dot(
        left, right, preferred_element_type=jnp.float32, precision=lax.Precision.HIGHEST
    )


def thirds(value):
    pieces = split3(value)
    size = value.shape[0]
    return [pieces[i * size : (i + 1) * size] for i in range(3)]


def wide(value):
    first, second, third = thirds(value)
    return jnp.concatenate([first, first, second, first, second, third], axis=1)


def tall(value):
    first, second, third = thirds(value)
    return jnp.concatenate([first, second, first, third, second, first], axis=0)


def eliminate(full, count):
    rows = lax.broadcasted_iota(jnp.int32, full.shape, 0)
    lanes = lax.broadcasted_iota(jnp.int32, full.shape, 1)
    for k in range(count):
        column = jnp.broadcast_to(full[:, k : k + 1], full.shape)
        row = full[k : k + 1, :] * (1.0 / column[k : k + 1, :])
        full = jnp.where(rows > k, full - column * row, full)
    pivots = jnp.sum(jnp.where(rows == lanes, full, 0.0), axis=1, keepdims=True)
    return full * (1.0 / jnp.sqrt(pivots))


def kernel(
    root_people,
    geno_hbm,
    freq_hbm,
    weight_hbm,
    basis_hbm,
    resid_hbm,
    block_hbm,
    comp_ref,
    coef_ref,
    next_ref,
    score_ref,
    geno,
    freq_ref,
    weight_ref,
    basis_ref,
    resid_ref,
    block_ref,
    dose,
    hot,
    perm,
    freq_rows,
    basis_rows,
    part,
    core_in,
    chip_part,
    chip_in,
    sketch_half,
    resid_score,
    resid_score_in,
    gram_part,
    gram_in,
    gram_sum,
    next_part,
    next_near,
    next_in,
    next_mine,
    next_pass,
    next_far,
    chosen_part,
    chosen_near,
    chosen_mine,
    chosen_pass,
    chosen_far,
    sketch_tall,
    geno_sem,
    load_sem,
    pair_send,
    pair_recv,
    send_sem,
    recv_sem,
):
    people = lax.axis_index("people")
    markers = lax.axis_index("markers")
    n = 4
    half = part.shape[1]
    k_count = 2 * half
    block = dose.shape[2]
    words = block // 4
    core = lax.rem(markers, 2)
    core_peer = markers + 1 - 2 * core
    chip_peer = lax.rem(markers + 2, n)
    people_peer = [people, people + 1 - 2 * lax.rem(people, 2), lax.rem(people + 2, n), 3 - people]
    starts = [sum(PIECES[:i]) for i in range(len(PIECES))]
    spans = [pl.ds(start, size) for start, size in zip(starts, PIECES)]

    loads = []
    for i, span in enumerate(spans):
        loads.append(pltpu.make_async_copy(geno_hbm.at[span], geno.at[span], geno_sem.at[i]))
    small = [
        pltpu.make_async_copy(src, dst, load_sem.at[i])
        for i, (src, dst) in enumerate(
            (
                (freq_hbm, freq_ref),
                (basis_hbm, basis_ref),
                (weight_hbm, weight_ref),
                (block_hbm, block_ref),
                (resid_hbm, resid_ref),
            )
        )
    ]
    for load in small[:3] + loads + small[3:]:
        load.start()

    barrier = pltpu.get_barrier_semaphore()
    for peer in (core_peer, chip_peer):
        pl.semaphore_signal(barrier, inc=1, device_id={"markers": peer}, device_id_type=MESH)
    for d in (1, 2, 3):
        pl.semaphore_signal(
            barrier, inc=1, device_id={"people": people_peer[d]}, device_id_type=MESH
        )

    sends = {}

    def send(group, d, src, dst):
        copy = pltpu.make_async_remote_copy(
            src_ref=src,
            dst_ref=dst,
            send_sem=send_sem.at[len(sends)],
            recv_sem=recv_sem.at[len(sends)],
            device_id={"people": people_peer[d]} if d else {"markers": core_peer},
            device_id_type=MESH,
        )
        copy.start()
        sends[group, d] = copy

    pairs = {}

    def pair(level, i):
        src, dst, peer = (
            (part.at[1 - core], core_in, core_peer),
            (chip_part, chip_in, chip_peer),
            (sketch_half.at[core], sketch_half.at[core], core_peer),
        )[level]
        copy = pltpu.make_async_remote_copy(
            src_ref=src.at[:, spans[i]],
            dst_ref=dst.at[:, spans[i]],
            send_sem=pair_send.at[level, i],
            recv_sem=pair_recv.at[level, i],
            device_id={"markers": peer},
            device_id_type=MESH,
        )
        copy.start()
        pairs[level, i] = copy

    place = lax.broadcasted_iota(jnp.int32, (1, block), 1)
    source = 4 * lax.rem(place, words) + lax.div(place, words)
    marker = lax.broadcasted_iota(jnp.int32, (block, block), 0)
    perm[...] = jnp.where(marker == source, 1.0, 0.0).astype(jnp.bfloat16)
    small[0].wait()
    small[1].wait()
    small[2].wait()
    freq = jnp.concatenate([freq_ref[:, c * block : (c + 1) * block] for c in range(n)], axis=0)
    freq = jnp.concatenate([freq, freq], axis=0)
    freq = sum3(mm(split3(freq), perm[...]))[:n]
    twice = 2.0 * freq
    scale = 1.0 / jnp.sqrt(2.0 * freq * (1.0 - freq))
    freq_rows[0:n, :] = twice
    freq_rows[n : 2 * n, :] = scale
    basis = jnp.concatenate([basis_ref[:, c * block : (c + 1) * block] for c in range(n)], axis=0)
    basis = mm(basis, perm[...])
    offset = jnp.zeros((k_count, 1), jnp.float32)
    for c in range(n):
        scaled = (basis[c * k_count : (c + 1) * k_count] * scale[c : c + 1]).astype(jnp.bfloat16)
        basis_rows[c] = scaled
        offset += jnp.sum(
            scaled.astype(jnp.float32) * twice[c : c + 1], axis=1, keepdims=True
        )
    weight = jnp.concatenate(
        [weight_ref[i : i + 1, :] for i in range(weight_ref.shape[0])], axis=1
    )

    def forward(i):
        pairs[0, i].wait_recv()
        chip_part[:, spans[i]] = part[core, :, spans[i]] + core_in[:, spans[i]]
        pair(1, i)

    def finish(i):
        pairs[1, i].wait_recv()
        sketch_half[core, :, spans[i]] = chip_part[:, spans[i]] + chip_in[:, spans[i]]
        pair(2, i)

    for i, span in enumerate(spans):
        loads[i].wait()
        total = None
        for c in range(n):
            packed = geno[span, c * words : (c + 1) * words]
            digits = [
                jnp.bitwise_and(packed, 3),
                jnp.bitwise_and(jnp.right_shift(packed, 2), 3),
                jnp.bitwise_and(jnp.right_shift(packed, 4), 3),
                jnp.right_shift(packed, 6),
            ]
            tile = jnp.concatenate(
                [digit.astype(jnp.float32).astype(jnp.bfloat16) for digit in digits], axis=1
            )
            dose[c, span, :] = tile
            got = mm_nt(basis_rows[c], tile)
            total = got if total is None else total + got
        value = (total - offset) * weight[:, starts[i] : starts[i] + PIECES[i]]
        part[0, :, span] = value[:half]
        part[1, :, span] = value[half:]
        if i == 0:
            pl.semaphore_wait(barrier, 5)
        pair(0, i)
        if i:
            forward(i - 1)

    small[3].wait()
    small[4].wait()
    local = block_ref[...] - markers * (n * block)
    inner = lax.rem(local, block)
    column = lax.div(local, block) * block + lax.rem(inner, 4) * words + lax.div(inner, 4)
    for c in range(n):
        row = lax.broadcasted_iota(jnp.int32, (block, hot.shape[2]), 0) + c * block
        hot[c] = jnp.where(row == column, 1.0, 0.0).astype(jnp.bfloat16)
    forward(len(PIECES) - 1)

    def center(raw, sums, c):
        return (raw - sums * freq_rows[c : c + 1, :]) * freq_rows[n + c : n + c + 1, :]

    resid = resid_ref[...]
    heavy = split2(resid.astype(jnp.float32) * weight)
    sums = sum2(jnp.sum(heavy.astype(jnp.float32), axis=1, keepdims=True))
    picked = None
    for c in range(n):
        value = center(sum2(mm(heavy, dose[c])), sums, c)
        got = mm(split2(value), hot[c])
        picked = got if picked is None else picked + got
    picked = sum2(picked)
    width = picked.shape[1] // n
    for c in range(n):
        resid_score[c] = picked[:, c * width : (c + 1) * width]
    for d in (2, 3, 1):
        send(0, d, resid_score.at[people_peer[d]], resid_score_in.at[d - 1])

    for i in range(len(PIECES)):
        finish(i)
    for i in range(len(PIECES)):
        pairs[2, i].wait_recv()
    sketch = jnp.concatenate([sketch_half[0], sketch_half[1]], axis=0)
    heavy = split2(sketch * weight)
    sums = sum2(jnp.sum(heavy.astype(jnp.float32), axis=1, keepdims=True))
    cut = block // 2
    picked = None
    for d in (3, 2, 1, 0):
        c = people_peer[d]
        freq_row = freq_rows[pl.ds(c, 1), :]
        scale_row = freq_rows[pl.ds(c + n, 1), :]
        sides = [None, None]
        for side in (1, 0):
            at = slice(side * cut, (side + 1) * cut)
            raw = sum2(mm(heavy, dose[c, :, at]))
            sides[side] = (raw - sums * freq_row[:, at]) * scale_row[:, at]
            next_part[c, side] = sides[side]
            if d == 3 and side:
                send(2, 1, next_part.at[c, 1], next_pass)
                pieces = split3(sketch)
                gram = sum3(mm_nt(pieces, jnp.concatenate([pieces, resid], axis=0)))
                square = (
                    gram[:, :k_count]
                    + gram[:, k_count : 2 * k_count]
                    + gram[:, 2 * k_count : 3 * k_count]
                )
                pad = jnp.zeros((k_count, k_count), jnp.float32)
                gram = jnp.concatenate([square, gram[:, 3 * k_count :], pad], axis=1)
                gram_part[0] = gram[:half]
                gram_part[1] = gram[half:]
                gram_in[people] = gram_part[core]
                for far in (3, 2, 1):
                    send(1, far, gram_part.at[core], gram_in.at[people])
        total = jnp.concatenate(sides, axis=1)
        if d > 1:
            send(2, d, next_part.at[c, 0], next_in.at[d - 2])
        got = mm(split2(total), hot[c])
        picked = got if picked is None else picked + got
    picked = sum2(picked)
    for c in range(n):
        chosen_part[c] = picked[:, c * width : (c + 1) * width]
    send(4, 1, chosen_part.at[people_peer[3]], chosen_pass)
    send(5, 1, chosen_part.at[people_peer[1]], chosen_near)

    sketch_tall[...] = tall(sketch)
    for copy in pairs.values():
        copy.wait_send()
    sends[2, 1].wait_recv()
    next_mine[...] = next_part[people_peer[2], 1] + next_pass[...]
    send(3, 2, next_mine, next_far)
    send(3, 1, next_part.at[people_peer[1]], next_near)
    for d in (1, 2, 3):
        sends[1, d].wait_recv()
    gram_sum[core] = gram_in[0] + gram_in[1] + gram_in[2] + gram_in[3]
    send(1, 0, gram_sum.at[core], gram_sum.at[core])
    sends[4, 1].wait_recv()
    chosen_mine[...] = chosen_part[people_peer[2]] + chosen_pass[...]
    send(4, 2, chosen_mine, chosen_far)
    sends[1, 0].wait_recv()
    full = jnp.concatenate([gram_sum[0], gram_sum[1]], axis=0)
    lane = lax.broadcasted_iota(jnp.int32, full.shape, 1)
    line = lax.broadcasted_iota(jnp.int32, full.shape, 0)
    full = jnp.where(lane == line + (TILE - k_count), 1.0, full)
    full = eliminate(full, k_count)
    coef = full[:, k_count : TILE - k_count]
    inverse = full[:, TILE - k_count :]
    coef_ref[...] = coef
    left = wide(inverse)
    comp_ref[...] = root_people * mm(left, sketch_tall[...])
    remover = lax.dot_general(
        coef,
        inverse,
        (((0,), (0,)), ((), ())),
        preferred_element_type=jnp.float32,
        precision=lax.Precision.HIGHEST,
    )

    for group, d in ((0, 1), (0, 2), (0, 3), (2, 2), (2, 3), (3, 1), (3, 2), (4, 2), (5, 1)):
        sends[group, d].wait_recv()
    total = next_part[people] + next_near[...]
    total = jnp.concatenate(
        [total[0] + next_in[0] + next_in[1], total[1] + next_far[...]], axis=1
    )
    chosen = chosen_part[people] + chosen_near[...] + chosen_far[...]
    scored = resid_score[people] + resid_score_in[0] + resid_score_in[1] + resid_score_in[2]
    solved = mm(left, tall(total))
    next_ref[0] = sum2(mm_nt(split2(solved), perm[...]))
    score_ref[0] = (scored - exact(remover, chosen)) * (1.0 / root_people)
    for copy in sends.values():
        copy.wait_send()


def write_results(*refs):
    sources, results, store_sem = refs[:4], refs[4:8], refs[8]
    stores = [pltpu.make_async_copy(sources[i], results[i], store_sem.at[i]) for i in range(4)]
    for store in stores:
        store.start()
    for store in stores:
        store.wait()


def fused(genotype, allele_freq, person_weight, basis, residuals, block_markers):
    n = 4
    rows, words = genotype.shape
    k_count = basis.shape[0]
    r_count = residuals.shape[0]
    block = 4 * words // n
    picks = block_markers.shape[0]
    width = picks // n
    f32, bf16 = jnp.float32, jnp.bfloat16
    hbm = pl.BlockSpec(memory_space=pltpu.HBM)
    vmem = pl.BlockSpec(memory_space=pltpu.VMEM)
    root_people = math.sqrt(rows * n)
    shapes = (
        jax.ShapeDtypeStruct((k_count, rows), f32),
        jax.ShapeDtypeStruct((k_count, r_count), f32),
        jax.ShapeDtypeStruct((1, k_count, block), f32),
        jax.ShapeDtypeStruct((1, r_count, width), f32),
    )
    results = pl.pallas_call(
        functools.partial(kernel, root_people),
        out_shape=tuple(pltpu.VMEM(shape.shape, shape.dtype) for shape in shapes),
        in_specs=[hbm] * 6,
        out_specs=(vmem,) * 4,
        scratch_shapes=[
            pltpu.VMEM((rows, words), jnp.int32),
            pltpu.VMEM((1, n * block), f32),
            pltpu.VMEM((rows // TILE, TILE), f32),
            pltpu.VMEM(basis.shape, bf16),
            pltpu.VMEM(residuals.shape, bf16),
            pltpu.VMEM((1, picks), jnp.int32),
            pltpu.VMEM((n, rows, block), bf16),
            pltpu.VMEM((n, block, picks), bf16),
            pltpu.VMEM((block, block), bf16),
            pltpu.VMEM((2 * n, block), f32),
            pltpu.VMEM((n, k_count, block), bf16),
            pltpu.VMEM((2, k_count // 2, rows), f32),
            pltpu.VMEM((k_count // 2, rows), f32),
            pltpu.VMEM((k_count // 2, rows), f32),
            pltpu.VMEM((k_count // 2, rows), f32),
            pltpu.VMEM((2, k_count // 2, rows), f32),
            pltpu.VMEM((n, r_count, width), f32),
            pltpu.VMEM((n - 1, r_count, width), f32),
            pltpu.VMEM((2, k_count // 2, TILE), f32),
            pltpu.VMEM((n, k_count // 2, TILE), f32),
            pltpu.VMEM((2, k_count // 2, TILE), f32),
            pltpu.VMEM((n, 2, k_count, block // 2), f32),
            pltpu.VMEM((2, k_count, block // 2), f32),
            pltpu.VMEM((2, k_count, block // 2), f32),
            pltpu.VMEM((k_count, block // 2), f32),
            pltpu.VMEM((k_count, block // 2), f32),
            pltpu.VMEM((k_count, block // 2), f32),
            pltpu.VMEM((n, k_count, width), f32),
            pltpu.VMEM((k_count, width), f32),
            pltpu.VMEM((k_count, width), f32),
            pltpu.VMEM((k_count, width), f32),
            pltpu.VMEM((k_count, width), f32),
            pltpu.VMEM((6 * k_count, rows), bf16),
            pltpu.SemaphoreType.DMA((len(PIECES),)),
            pltpu.SemaphoreType.DMA((5,)),
            pltpu.SemaphoreType.DMA((3, len(PIECES))),
            pltpu.SemaphoreType.DMA((3, len(PIECES))),
            pltpu.SemaphoreType.DMA((16,)),
            pltpu.SemaphoreType.DMA((16,)),
        ],
        compiler_params=pltpu.CompilerParams(
            collective_id=0, has_side_effects=True, vmem_limit_bytes=62 * 2**20
        ),
    )(
        genotype,
        allele_freq.reshape(1, -1),
        person_weight.reshape(-1, TILE),
        basis,
        residuals,
        block_markers.reshape(1, -1),
    )
    return pl.pallas_call(
        write_results,
        out_shape=shapes,
        in_specs=[vmem] * 4,
        out_specs=(hbm,) * 4,
        scratch_shapes=[pltpu.SemaphoreType.DMA((4,))],
    )(*[pltpu.with_memory_space_constraint(r, pltpu.VMEM) for r in results])


def solution(mesh):
    small = mesh.shape["people"] == 4 and mesh.shape["markers"] == 4
    placed = (
        P(("cohort", "people"), "markers"),
        P(("cohort", "markers")),
        P(("cohort", "people")),
        P("cohort", "markers"),
        P("cohort", "people"),
        P("markers"),
    )
    return jax.shard_map(
        fused if small else shards,
        mesh=mesh,
        in_specs=placed,
        out_specs=(
            P("cohort", "people"),
            P("cohort", None),
            P("markers", "cohort", "people"),
            P("markers", "cohort", "people"),
        ),
        check_vma=False,
    )
```
